256 devices in a mesh: grp: 8 (over z), seq: 32 (over y, x, core).
Axes of the slice: x: 4, y: 4, z: 8, core: 2. Of those that a mesh axis runs over, the one named last changes fastest.
Arguments:
- cache_hidden: bfloat16 [16384, 5120], P(('grp', 'seq')), parts along dimension 0, may hold values from -12 to 12
- group_hidden: bfloat16 [2048, 5120], P(('grp', 'seq')), parts along dimension 0, may hold values from -12 to 12
- proj_weight: bfloat16 [5120, 32, 3, 128], P(None, 'seq'), may hold values from -1 to 1
- row_place: int32 [16384], P(('grp', 'seq')), parts along dimension 0, may hold values from 0 to 2047, as said below
- cache_len: int32 [256], P('grp'), parts along dimension 0, may hold values from 1 to 64, as said below
- group_place: int32 [2048], P(('grp', 'seq')), parts along dimension 0, may hold values from 0 to 255, each once
Outputs:
- attended: bfloat16 [2048, 4096], P(('grp', 'seq')), parts along dimension 0
The draws below stay inside these ranges and needn't reach their ends.
There are 8 independent parts, one for each index of `grp`. The reference program is written for one: setup_inputs(seed, part) draws one part's arguments, and reference() takes and returns one part's arrays. A program takes and returns all parts, laid end to end along the dimension named above; an argument that names none is the same for every part. Nothing has to cross between parts.
Inputs may be any that keep to these rules, and one draw needn't show every extreme that they name: `row_place`: each session position appears exactly once; the 64 rows of every device hold exactly 48 live positions. `cache_len`: the lengths sum to 1536; some owner full. `group_place`: each turn position appears exactly once.
All inputs are finite; a program needn't handle non-finite values.
Results may differ from the reference program's by a relative error of at most 0.009.
Values may be sent and summed in bfloat16 or wider, within the bound.
No kernel may reach another device: no remote copies, remote signals or barrier semaphores. Data moves between devices by JAX's collectives and lax.ppermute only.
A program may use at most 128 MiB of HBM per device.

```python
import math
import jax
import jax.numpy as jnp
from jax import lax

D = 5120
HEAD_DIM = 128
CACHE_DEV = 64
LIVE_DEV = 48
HEADS = 32
OWNERS = 32
SESSION = 2048
GROUP = 256


def shared_rows(key):
    gauss_rows = jnp.clip(jax.random.normal(key, (SESSION, D), jnp.float32), -6.0, 6.0)
    return gauss_rows


def placement_draw(key):
    owner_order = jax.random.permutation(jax.random.fold_in(key, 21), OWNERS)
    pairs = OWNERS // 2
    span = CACHE_DEV - LIVE_DEV
    shifts = jax.random.randint(jax.random.fold_in(key, 22), (pairs,), -span, span + 1).astype(jnp.int32)
    shifts = shifts.at[0].set(span)
    delta = jnp.zeros((OWNERS,), jnp.int32).at[owner_order[0::2]].set(shifts).at[owner_order[1::2]].set(-shifts)
    lengths = (LIVE_DEV + delta).astype(jnp.int32)
    positions = jnp.arange(SESSION, dtype=jnp.int32)
    dead = (positions % CACHE_DEV >= lengths[positions // CACHE_DEV]).astype(jnp.int32)
    ranks = jax.random.permutation(jax.random.fold_in(key, 23), SESSION).astype(jnp.int32)
    order = jnp.argsort(dead * SESSION + ranks).astype(jnp.int32)
    live_total = OWNERS * LIVE_DEV
    block = positions // CACHE_DEV
    inner = positions % CACHE_DEV
    pick = jnp.where(inner < LIVE_DEV, block * LIVE_DEV + inner, live_total + block * span + inner - LIVE_DEV)
    placed = order[pick]
    mixing = jax.random.permutation(jax.random.fold_in(key, 24), SESSION).astype(jnp.int32)
    shuffle = jnp.argsort(block * SESSION + mixing).astype(jnp.int32)
    return (lengths, placed[shuffle].astype(jnp.int32))


def draw_row_place(key, part):
    lengths, places = placement_draw(key)
    return places


def draw_cache_len(key, part):
    lengths, places = placement_draw(key)
    return lengths


def draw_cache_hidden(key, part):
    gauss_rows = shared_rows(key)
    return gauss_rows.astype(jnp.bfloat16)


def draw_group_hidden(key, part):
    key = jax.random.fold_in(key, 4)
    own_rows = jnp.clip(jax.random.normal(key, (GROUP, D), jnp.float32), -6.0, 6.0)
    return own_rows.astype(jnp.bfloat16)


def draw_proj_weight(key, part):
    key = jax.random.fold_in(key, 5)
    gauss_rows = jnp.clip(jax.random.normal(key, (D, HEADS, 3, HEAD_DIM), jnp.float32), -6.0, 6.0)
    return (gauss_rows / math.sqrt(D)).astype(jnp.bfloat16)


def setup_inputs(seed: int = 0, part: int = 0) -> dict:
    splits = jax.random.split(jax.random.key(seed), 7)
    own_keys = jax.random.split(jax.random.fold_in(splits[6], part), 7)
    cache_hidden = draw_cache_hidden(jax.random.fold_in(jax.random.fold_in(splits[6], part), 71), part)
    group_hidden = draw_group_hidden(jax.random.fold_in(jax.random.fold_in(splits[6], part), 71), part)
    proj_weight = draw_proj_weight(jax.random.fold_in(splits[6], 71), part)
    row_place = draw_row_place(jax.random.fold_in(jax.random.fold_in(splits[6], part), 71), part)
    cache_len = draw_cache_len(jax.random.fold_in(jax.random.fold_in(splits[6], part), 71), part)
    group_place = jax.random.permutation(own_keys[5], GROUP).astype(jnp.int32)
    return dict(cache_hidden=cache_hidden, group_hidden=group_hidden, proj_weight=proj_weight, row_place=row_place, cache_len=cache_len, group_place=group_place)


MASKED_SCORE = -1.0e30


def reference(cache_hidden, group_hidden, proj_weight, row_place, cache_len, group_place):
    score_scale = HEAD_DIM ** -0.5
    kv_weight = proj_weight[:, :, 1:, :].reshape(D, HEADS * 2 * HEAD_DIM)
    moved_kv = jnp.dot(cache_hidden, kv_weight, preferred_element_type=jnp.float32).astype(jnp.bfloat16)
    moved_kv = moved_kv.reshape(SESSION, HEADS, 2, HEAD_DIM)
    restored = jnp.zeros_like(moved_kv).at[row_place].set(moved_kv)
    all_weight = proj_weight.reshape(D, HEADS * 3 * HEAD_DIM)
    fresh_qkv = jnp.dot(group_hidden, all_weight, preferred_element_type=jnp.float32).astype(jnp.bfloat16)
    fresh_qkv = fresh_qkv.reshape(GROUP, HEADS, 3, HEAD_DIM)
    positions = jnp.arange(SESSION, dtype=jnp.int32)
    live_keys = (positions % CACHE_DEV) < cache_len[positions // CACHE_DEV]
    seen_keys = group_place[None, :] <= group_place[:, None]
    visible = jnp.concatenate([jnp.broadcast_to(live_keys[None, :], (GROUP, SESSION)), seen_keys], axis=1)

    def one_head(head):
        queries = fresh_qkv[:, head, 0]
        key_rows = jnp.concatenate([restored[:, head, 0], fresh_qkv[:, head, 1]], axis=0)
        value_rows = jnp.concatenate([restored[:, head, 1], fresh_qkv[:, head, 2]], axis=0)
        scores = jnp.dot(queries, key_rows.T, preferred_element_type=jnp.float32) * score_scale
        scores = jnp.where(visible, scores, MASKED_SCORE)
        row_top = jnp.max(scores, axis=1, keepdims=True)
        weights = jnp.exp(scores - row_top)
        row_total = jnp.sum(weights, axis=1, keepdims=True)
        rounded = weights.astype(jnp.bfloat16)
        summed = jnp.dot(rounded, value_rows, preferred_element_type=jnp.float32)
        return (summed / row_total).astype(jnp.bfloat16)

    per_head = lax.map(one_head, jnp.arange(HEADS, dtype=jnp.int32))
    return jnp.transpose(per_head, (1, 0, 2)).reshape(GROUP, HEADS * HEAD_DIM)
```

```python
import functools

import jax
import jax.numpy as jnp
import numpy as np
from jax import lax
from jax.experimental import pallas as pl
from jax.experimental.pallas import tpu as pltpu
from jax.sharding import PartitionSpec as P

MASKED_SCORE = -1e30
NY, NX = 4, 4
LIVE = 48
HD = 128
TURN = 8
BF16 = jnp.bfloat16
F32 = jnp.float32


def index_of(y, x, c):
    return (y % NY * NX + x % NX) * 2 + c


def ring_pairs(step, first):
    pairs = []
    for y in range(NY):
        for x in range(NX):
            for c in range(2):
                along_x = (c == 0) == first
                dy, dx = (0, step) if along_x else (step, 0)
                pairs.append((index_of(y, x, c), index_of(y + dy, x + dx, c)))
    return pairs


A_UP, A_DOWN = ring_pairs(1, True), ring_pairs(-1, True)
B_UP, B_DOWN = ring_pairs(1, False), ring_pairs(-1, False)
SWAP = [(i, i ^ 1) for i in range(2 * NY * NX)]
OFFSETS = (0, -1, 1, -2)


def token_owner_table():
    table = np.zeros((2 * NY * NX, 2 * NY * NX), np.int32)
    for y in range(NY):
        for x in range(NX):
            for c in range(2):
                row = []
                for core in (c, 1 - c):
                    for b in OFFSETS:
                        for a in OFFSETS:
                            dy, dx = (b, a) if core == 0 else (a, b)
                            row.append(index_of(y + dy, x + dx, core))
                table[index_of(y, x, c)] = row
    return table


def send(value, pairs):
    return lax.ppermute(value, "seq", pairs)


def pack_kernel(place_ref, len_ref, rows_ref, out_ref):
    n = rows_ref.shape[0]
    block = n
    i0 = lax.broadcasted_iota(jnp.int32, (n, n), 0)
    i1 = lax.broadcasted_iota(jnp.int32, (n, n), 1)
    place_col = jnp.sum(jnp.where(i0 == i1, place_ref[...], 0), axis=1, keepdims=True)
    owner = place_col // block
    inner = place_col - owner * block
    owners = len_ref.shape[1]
    o1 = lax.broadcasted_iota(jnp.int32, (n, owners), 1)
    length = jnp.sum(jnp.where(o1 == owner, len_ref[...], 0), axis=1, keepdims=True)
    live_col = (inner < length).astype(jnp.int32)
    live_row = jnp.sum(jnp.where(i0 == i1, live_col, 0), axis=0, keepdims=True)
    rank_row = jnp.sum(jnp.where(i0 < i1, live_col, 0), axis=0, keepdims=True)
    k0 = lax.broadcasted_iota(jnp.int32, (LIVE, n), 0)
    pick = jnp.where((k0 == rank_row) & (live_row > 0), 1.0, 0.0).astype(BF16)
    out_ref[...] = jnp.dot(pick, rows_ref[...], preferred_element_type=F32).astype(BF16)


def pack(row_place, cache_len, cache_hidden):
    n, d = cache_hidden.shape
    return pl.pallas_call(
        pack_kernel,
        out_shape=jax.ShapeDtypeStruct((LIVE, d), BF16),
        cost_estimate=pl.CostEstimate(flops=2 * n * LIVE * d, bytes_accessed=4 * n * d, transcendentals=0),
        name="pack_live",
    )(row_place.reshape(1, n), cache_len.reshape(1, -1), cache_hidden)


def turn_kernel(a, b, c, d, pa, pb, pc, pd, own_ref, other_ref, q_ref, kv_ref, acc):
    k = pl.program_id(0)

    @pl.when(k == 0)
    def _():
        acc[...] = jnp.zeros_like(acc)

    x = jnp.concatenate([a[...], b[...], c[...], d[...]], axis=0)
    w = jnp.concatenate(
        [own_ref[0], other_ref[0], own_ref[1], own_ref[2], other_ref[1], other_ref[2]], axis=1
    )
    acc[...] += jnp.dot(x, w, preferred_element_type=F32)

    @pl.when(k == pl.num_programs(0) - 1)
    def _():
        q_ref[:, : 2 * HD] = acc[:, : 2 * HD].astype(BF16)
        q_ref[:, 2 * HD :] = jnp.concatenate([pa[...], pb[...], pc[...], pd[...]], axis=0)
        kv_ref[...] = acc[:, 2 * HD :].astype(BF16)


def turn_project(blocks, own, other, kb=1024):
    m = blocks[0].shape[0]
    d = own.shape[1]
    xs = pl.BlockSpec((m, kb), lambda k: (0, k))
    ps = pl.BlockSpec((m, HD), lambda k: (0, d // HD))
    ws = pl.BlockSpec((3, kb, HD), lambda k: (0, k, 0))
    return pl.pallas_call(
        turn_kernel,
        grid=(d // kb,),
        in_specs=[xs] * 4 + [ps] * 4 + [ws] * 2,
        out_specs=[
            pl.BlockSpec((4 * m, 3 * HD), lambda k: (0, 0)),
            pl.BlockSpec((4 * m, 4 * HD), lambda k: (0, 0)),
        ],
        out_shape=[
            jax.ShapeDtypeStruct((4 * m, 3 * HD), BF16),
            jax.ShapeDtypeStruct((4 * m, 4 * HD), BF16),
        ],
        scratch_shapes=[pltpu.VMEM((4 * m, 6 * HD), F32)],
        compiler_params=pltpu.CompilerParams(vmem_limit_bytes=24 * 2**20),
        cost_estimate=pl.CostEstimate(
            flops=2 * 4 * m * d * 6 * HD, bytes_accessed=2 * d * (4 * m + 6 * HD), transcendentals=0
        ),
        name="project_turn",
    )(*blocks, *blocks, own, other)


def cache_kernel(a, b, c, d, own_ref, other_ref, kv_ref, acc):
    k = pl.program_id(0)

    @pl.when(k == 0)
    def _():
        acc[...] = jnp.zeros_like(acc)

    x = jnp.concatenate([a[...], b[...], c[...], d[...]], axis=0)
    w = jnp.concatenate([own_ref[0], own_ref[1], other_ref[0], other_ref[1]], axis=1)
    acc[...] += jnp.dot(x, w, preferred_element_type=F32)

    @pl.when(k == pl.num_programs(0) - 1)
    def _():
        kv_ref[...] = acc[...].astype(BF16)


def cache_project(shards, own, other, kb=1024):
    m, d = shards[0].shape
    xs = pl.BlockSpec((m, kb), lambda k: (0, k))
    ws = [
        pl.BlockSpec((pl.Element(2), pl.Element(kb), pl.Element(HD)), lambda k: (1, k * kb, 0))
        for _ in range(2)
    ]
    return pl.pallas_call(
        cache_kernel,
        grid=(d // kb,),
        in_specs=[xs] * 4 + ws,
        out_specs=pl.BlockSpec((4 * m, 4 * HD), lambda k: (0, 0)),
        out_shape=jax.ShapeDtypeStruct((4 * m, 4 * HD), BF16),
        scratch_shapes=[pltpu.VMEM((4 * m, 4 * HD), F32)],
        compiler_params=pltpu.CompilerParams(vmem_limit_bytes=24 * 2**20),
        cost_estimate=pl.CostEstimate(
            flops=2 * 4 * m * d * 4 * HD, bytes_accessed=2 * d * (4 * m + 4 * HD), transcendentals=0
        ),
        name="project_cache",
    )(*shards, own, other)


def attend_kernel(core_ref, dest_ref, q_ref, qs_ref, kvf_ref, k0, k1, k2, k3, out_ref):
    core = core_ref[0]
    q_place = jnp.concatenate([q_ref[:, 2 * HD :], qs_ref[:, 2 * HD :]], axis=0).astype(F32)
    k_place = q_ref[:, 2 * HD :].astype(F32).T[0:1, :]
    seen = k_place <= q_place[:, 0:1]
    outs, tops, totals = [], [], []
    for h in range(2):
        q = jnp.concatenate(
            [q_ref[:, h * HD : (h + 1) * HD], qs_ref[:, (1 - h) * HD : (2 - h) * HD]], axis=0
        )
        ks = slice(2 * h * HD, (2 * h + 1) * HD)
        vs = slice((2 * h + 1) * HD, (2 * h + 2) * HD)
        scale = HD ** (-0.5)
        nt = (((1,), (1,)), ((), ()))
        s = [
            lax.dot_general(q, r[:, ks], nt, preferred_element_type=F32) * scale
            for r in (k0, k1, k2, k3)
        ]
        f = lax.dot_general(q, kvf_ref[:, ks], nt, preferred_element_type=F32) * scale
        s.append(jnp.where(seen, f, MASKED_SCORE))
        top = functools.reduce(
            jnp.maximum, [jnp.max(t, axis=1, keepdims=True) for t in s]
        )
        total = jnp.zeros_like(top)
        summed = jnp.zeros((q.shape[0], HD), F32)
        for t, r in zip(s, (k0, k1, k2, k3, kvf_ref)):
            e = jnp.exp(t - top)
            total += jnp.sum(e, axis=1, keepdims=True)
            summed += jnp.dot(e.astype(BF16), r[:, vs], preferred_element_type=F32)
        outs.append(summed)
        tops.append(top)
        totals.append(total)
    first = core == 0
    lane = lax.broadcasted_iota(jnp.int32, (outs[0].shape[0], HD), 1)
    stats = []
    for h in range(2):
        stats.append(jnp.where(lane % 64 < 32, tops[h], totals[h]))
    low = jnp.where(first, outs[0], outs[1])
    high = jnp.where(first, outs[1], outs[0])
    stat = jnp.where(
        lane < 64, jnp.where(first, stats[0], stats[1]), jnp.where(first, stats[1], stats[0])
    )
    whole = jnp.concatenate([low, high, stat], axis=1)
    for g in range(out_ref.shape[0]):
        out_ref[dest_ref[g]] = whole[g * TURN : (g + 1) * TURN]


def attend(core, dest, q, q_swapped, kv_turn, kv_cache):
    n = dest.shape[0]
    smem = pl.BlockSpec(memory_space=pltpu.SMEM)
    vmem = pl.BlockSpec(memory_space=pltpu.VMEM)
    keys = 128 + 4 * 192
    return pl.pallas_call(
        attend_kernel,
        in_specs=[smem, smem] + [vmem] * 7,
        out_specs=vmem,
        out_shape=jax.ShapeDtypeStruct((n, TURN, 3 * HD), F32),
        compiler_params=pltpu.CompilerParams(vmem_limit_bytes=24 * 2**20),
        cost_estimate=pl.CostEstimate(
            flops=2 * 2 * 2 * 256 * keys * HD, bytes_accessed=2 * 2**20, transcendentals=2 * 256 * keys
        ),
        name="attend",
    )(core, dest, q, q_swapped, kv_turn, *kv_cache)


def combine_kernel(in_ref, out_ref):
    for j in range(in_ref.shape[0] // 2):
        for h in range(2):
            cols = slice(h * HD, (h + 1) * HD)
            at = 2 * HD + 64 * h
            o0, o1 = in_ref[2 * j, :, cols], in_ref[2 * j + 1, :, cols]
            m0, m1 = in_ref[2 * j, :, at : at + 1], in_ref[2 * j + 1, :, at : at + 1]
            l0, l1 = in_ref[2 * j, :, at + 32 : at + 33], in_ref[2 * j + 1, :, at + 32 : at + 33]
            top = jnp.maximum(m0, m1)
            e0, e1 = jnp.exp(m0 - top), jnp.exp(m1 - top)
            out = (o0 * e0 + o1 * e1) / (l0 * e0 + l1 * e1)
            out_ref[:, (2 * j + h) * HD : (2 * j + h + 1) * HD] = out.astype(BF16)


def combine(parts):
    n, t, _ = parts.shape
    return pl.pallas_call(
        combine_kernel,
        out_shape=jax.ShapeDtypeStruct((t, n * HD), BF16),
        cost_estimate=pl.CostEstimate(flops=n * t * HD * 8, bytes_accessed=n * t * HD * 14, transcendentals=n * t),
        name="combine",
    )(parts)


def shards(cache_hidden, group_hidden, proj_weight, row_place, cache_len, group_place):
    me = lax.axis_index("seq")
    dest = lax.dynamic_index_in_dim(jnp.asarray(token_owner_table()), me, 0, keepdims=False)
    core = (me % 2).astype(jnp.int32).reshape(1)

    places = jnp.broadcast_to(group_place.astype(BF16)[:, None], (group_place.shape[0], HD))
    g = jnp.concatenate([group_hidden, places], axis=1)
    own = jnp.transpose(proj_weight[:, 0], (1, 0, 2))
    other = send(own, SWAP)

    g_up, g_down = send(g, A_UP), send(g, A_DOWN)
    block = jnp.concatenate([g, g_up, g_down, send(g_up, A_UP)], axis=0)
    b_up, b_down = send(block, B_UP), send(block, B_DOWN)
    q, kv_turn = turn_project([block, b_up, b_down, send(b_up, B_UP)], own, other)
    q_swapped = send(q, SWAP)

    s = pack(row_place, cache_len, cache_hidden)
    half = LIVE // 2
    up, down = send(s, A_UP), send(s, A_DOWN)
    far = jnp.concatenate([send(up[:half], A_UP), send(down[half:], A_DOWN)], axis=0)
    near = [s, up, down, far]
    ups = [send(v, B_UP) for v in near]
    downs = [send(v, B_DOWN) for v in near]
    fars = [send(v, B_UP) for v in ups[:2]] + [send(v, B_DOWN) for v in downs[2:]]
    kv = [cache_project(v, own, other) for v in (near, ups, downs, fars)]

    parts = attend(core, dest, q, q_swapped, kv_turn, kv)
    landed = lax.all_to_all(parts, "seq", split_axis=0, concat_axis=0, tiled=True)
    return combine(landed)


def solution(mesh):
    in_specs = (
        P(("grp", "seq"), None),
        P(("grp", "seq"), None),
        P(None, "seq", None, None),
        P(("grp", "seq")),
        P("grp"),
        P(("grp", "seq")),
    )
    out_specs = P(("grp", "seq"), None)
    return jax.shard_map(shards, mesh=mesh, in_specs=in_specs, out_specs=out_specs, check_vma=False)
```

```python
import functools

import jax
import jax.numpy as jnp
from jax import lax
from jax.experimental import pallas as pl
from jax.experimental.pallas import tpu as pltpu
from jax.sharding import PartitionSpec as P

MASKED_SCORE = -1e30
NY, NX = 4, 4
LIVE = 48
HD = 128
TURN = 8
HALF = LIVE // 2
QUAD = TURN // 2
BF16 = jnp.bfloat16
F32 = jnp.float32


def index_of(y, x, c):
    return (y % NY * NX + x % NX) * 2 + c


def ring_pairs(step, first):
    pairs = []
    for y in range(NY):
        for x in range(NX):
            for c in range(2):
                along_x = (c == 0) == first
                dy, dx = (0, step) if along_x else (step, 0)
                pairs.append((index_of(y, x, c), index_of(y + dy, x + dx, c)))
    return pairs


A_UP, A_DOWN = ring_pairs(1, True), ring_pairs(-1, True)
B_UP, B_DOWN = ring_pairs(1, False), ring_pairs(-1, False)
SWAP = [(i, i ^ 1) for i in range(2 * NY * NX)]
OFFSETS = (0, -1, 1, -2)


def token_owner(me, group):
    core = lax.rem(me, 2)
    y, x = lax.div(me, 2 * NX), lax.rem(lax.div(me, 2), NX)
    along_x = core == 0
    if group >= NX * NY:
        core, along_x = 1 - core, core == 1
    b, a = OFFSETS[group % (NX * NY) // 4], OFFSETS[group % 4]
    dy, dx = jnp.where(along_x, b, a), jnp.where(along_x, a, b)
    return (lax.rem(y + dy + NY, NY) * NX + lax.rem(x + dx + NX, NX)) * 2 + core


def send(value, pairs):
    return lax.ppermute(value, "seq", pairs)


VMEM = pl.BlockSpec(memory_space=pltpu.VMEM)


def limit(mib):
    return pltpu.CompilerParams(vmem_limit_bytes=mib * 2**20)


def pack_kernel(*refs):
    sources, (one_ref, two_ref), scratch, sems = refs[:5], refs[5:7], refs[7:12], refs[12]
    copies = [pltpu.make_async_copy(a, b, sems.at[i]) for i, (a, b) in enumerate(zip(sources, scratch))]
    for copy in copies:
        copy.start()
    for copy in copies:
        copy.wait()
    place_ref, len_ref, turn_place_ref, rows_ref, turn_ref = scratch
    n, d = rows_ref.shape
    i0 = lax.broadcasted_iota(jnp.int32, (n, n), 0)
    i1 = lax.broadcasted_iota(jnp.int32, (n, n), 1)
    place_col = jnp.sum(jnp.where(i0 == i1, place_ref[...], 0), axis=1, keepdims=True)
    owner = place_col // n
    inner = place_col - owner * n
    o1 = lax.broadcasted_iota(jnp.int32, (n, len_ref.shape[1]), 1)
    length = jnp.sum(jnp.where(o1 == owner, len_ref[...], 0), axis=1, keepdims=True)
    live_col = (inner < length).astype(jnp.int32)
    live_row = jnp.sum(jnp.where(i0 == i1, live_col, 0), axis=0, keepdims=True)
    rank_row = jnp.sum(jnp.where(i0 < i1, live_col, 0), axis=0, keepdims=True)
    rank_row = jnp.where(live_row > 0, rank_row, -1)
    k0 = lax.broadcasted_iota(jnp.int32, (LIVE, n), 0)
    pick = jnp.where(k0 == rank_row, 1.0, 0.0).astype(BF16)
    live = jnp.dot(pick, rows_ref[...], preferred_element_type=F32)
    turn = turn_ref[...].astype(F32)
    m = HALF + QUAD
    t0 = lax.broadcasted_iota(jnp.int32, (m, TURN), 0)
    t1 = lax.broadcasted_iota(jnp.int32, (m, TURN), 1)
    for i, ref in enumerate((one_ref, two_ref)):
        rows, quad = live[i * HALF : (i + 1) * HALF], turn[i * QUAD : (i + 1) * QUAD]
        ref[:, :d] = jnp.concatenate([rows, quad], axis=0).astype(BF16)
        mine = t0 - HALF + i * QUAD == t1
        turn_col = jnp.sum(jnp.where(mine, turn_place_ref[...], 0), axis=1, keepdims=True)
        ref[:, d:] = jnp.broadcast_to(turn_col.astype(F32), (m, HD)).astype(BF16)


def pack(row_place, cache_len, group_place, cache_hidden, group_hidden):
    n, d = cache_hidden.shape
    m = HALF + QUAD
    args = (row_place.reshape(1, n), cache_len.reshape(1, -1), group_place.reshape(1, -1), cache_hidden, group_hidden)
    return pl.pallas_call(
        pack_kernel,
        in_specs=[pl.BlockSpec(memory_space=pl.ANY)] * 5,
        out_specs=[VMEM] * 2,
        out_shape=[jax.ShapeDtypeStruct((m, d + HD), BF16)] * 2,
        scratch_shapes=[pltpu.VMEM(v.shape, v.dtype) for v in args] + [pltpu.SemaphoreType.DMA((5,))],
        compiler_params=limit(56),
        cost_estimate=pl.CostEstimate(flops=2 * n * LIVE * d, bytes_accessed=4 * n * d, transcendentals=0),
        name="pack_live",
    )(*args)


def join_kernel(a, b, c, e, out_ref):
    x = [r[...].astype(F32) for r in (a, b, c, e)]
    out_ref[: 4 * HALF] = jnp.concatenate([v[:HALF] for v in x], axis=0).astype(BF16)
    out_ref[4 * HALF :] = jnp.concatenate([v[HALF:] for v in x], axis=0).astype(BF16)


def join(parts):
    m, w = parts[0].shape
    return pl.pallas_call(
        join_kernel,
        in_specs=[VMEM] * 4,
        out_specs=VMEM,
        out_shape=jax.ShapeDtypeStruct((4 * m, w), BF16),
        compiler_params=limit(8),
        cost_estimate=pl.CostEstimate(flops=0, bytes_accessed=16 * m * w, transcendentals=0),
        name="join_shards",
    )(*parts)


def project_rows(refs, own_ref, other_ref):
    d = own_ref.shape[1]
    x = jnp.concatenate([r[: 4 * HALF, :d] for r in refs], axis=0)
    w = jnp.concatenate([own_ref[1], own_ref[2], other_ref[1], other_ref[2]], axis=1)
    return jnp.dot(x, w, preferred_element_type=F32).astype(BF16)


def turn_kernel(*refs):
    *blocks, own_ref, other_ref, q_ref, kv_ref = refs
    d = own_ref.shape[1]
    turns = jnp.concatenate([r[4 * HALF :] for r in blocks], axis=0)
    x, places = turns[:, :d], turns[:, d:]
    w = jnp.concatenate([r[i] for r in (own_ref, other_ref) for i in range(3)], axis=1)
    qkv = jnp.dot(x, w, preferred_element_type=F32).astype(BF16)
    n = x.shape[0]
    to = lax.broadcasted_iota(jnp.int32, (n, n), 0)
    source = to - to % 32 + to % 8 // QUAD * 16 + to % 32 // 8 * QUAD + to % QUAD
    order = jnp.where(source == lax.broadcasted_iota(jnp.int32, (n, n), 1), 1.0, 0.0).astype(BF16)
    both = jnp.concatenate([qkv, places], axis=1)
    both = jnp.dot(order, both, preferred_element_type=F32).astype(BF16)
    q_ref[:, :HD] = both[:, :HD]
    q_ref[:, HD : 2 * HD] = both[:, 3 * HD : 4 * HD]
    q_ref[:, 2 * HD :] = both[:, 6 * HD :]
    kv_ref[:, : 2 * HD] = both[:, HD : 3 * HD]
    kv_ref[:, 2 * HD :] = both[:, 4 * HD : 6 * HD]


def turn_project(blocks, own, other):
    m, d = 4 * QUAD * len(blocks), own.shape[1]
    return pl.pallas_call(
        turn_kernel,
        in_specs=[VMEM] * (len(blocks) + 2),
        out_specs=[VMEM] * 2,
        out_shape=[
            jax.ShapeDtypeStruct((m, 3 * HD), BF16),
            jax.ShapeDtypeStruct((m, 4 * HD), BF16),
        ],
        compiler_params=limit(16),
        cost_estimate=pl.CostEstimate(flops=2 * m * d * 6 * HD * 3, bytes_accessed=2**20, transcendentals=0),
        name="project_turn",
    )(*blocks, own, other)


def cache_kernel(*refs):
    *rows, own_ref, other_ref, kv_ref = refs
    kv_ref[...] = project_rows(rows, own_ref, other_ref)


def cache_project(rows, own, other):
    m, d = 4 * HALF * len(rows), own.shape[1]
    return pl.pallas_call(
        cache_kernel,
        in_specs=[VMEM] * (len(rows) + 2),
        out_specs=VMEM,
        out_shape=jax.ShapeDtypeStruct((m, 4 * HD), BF16),
        compiler_params=limit(16),
        cost_estimate=pl.CostEstimate(flops=2 * m * d * 4 * HD * 3, bytes_accessed=2**20, transcendentals=0),
        name="project_cache",
    )(*rows, own, other)


def terms(x):
    hi = x.astype(BF16).astype(F32)
    mid = (x - hi).astype(BF16).astype(F32)
    return [hi, mid, x - hi - mid]


def attend_kernel(qa_ref, qb_ref, qsa_ref, qsb_ref, kva_ref, kvb_ref, k0, k1, k2, out_ref):
    me = lax.axis_index("seq")
    first = lax.rem(me, 2) == 0
    mine = jnp.concatenate([qa_ref[...], qb_ref[...]], axis=0)
    theirs = jnp.concatenate([qsa_ref[...], qsb_ref[...]], axis=0)
    fresh = jnp.concatenate([kva_ref[...], kvb_ref[...]], axis=0)
    q_place = jnp.concatenate([mine[:, 2 * HD :], theirs[:, 2 * HD :]], axis=0).astype(F32)
    k_place = mine[:, 2 * HD :].astype(F32).T[0:1, :]
    seen = k_place <= q_place[:, 0:1]
    scale = HD ** (-0.5)
    nt = (((1,), (1,)), ((), ()))
    outs, stats = [], []
    lane = lax.broadcasted_iota(jnp.int32, (q_place.shape[0], HD), 1) % 64
    for h in range(2):
        q = jnp.concatenate(
            [mine[:, h * HD : (h + 1) * HD], theirs[:, (1 - h) * HD : (2 - h) * HD]], axis=0
        )
        ks = slice(2 * h * HD, (2 * h + 1) * HD)
        vs = slice((2 * h + 1) * HD, (2 * h + 2) * HD)
        s = [
            lax.dot_general(q, r[:, ks], nt, preferred_element_type=F32) * scale
            for r in (k0, k1, k2)
        ]
        f = lax.dot_general(q, fresh[:, ks], nt, preferred_element_type=F32) * scale
        s.append(jnp.where(seen, f, MASKED_SCORE))
        top = functools.reduce(jnp.maximum, [jnp.max(t, axis=1, keepdims=True) for t in s])
        total = jnp.zeros_like(top)
        summed = jnp.zeros((q.shape[0], HD), F32)
        for t, r in zip(s, (k0, k1, k2, fresh)):
            e = jnp.exp(t - top)
            total += jnp.sum(e, axis=1, keepdims=True)
            summed += jnp.dot(e.astype(BF16), r[:, vs], preferred_element_type=F32)
        outs.append(summed)
        stat = jnp.zeros((q.shape[0], HD), F32)
        for i, v in enumerate(terms(top) + terms(total)):
            stat = jnp.where(lane // 8 == i, v, stat)
        stats.append(stat)
    low = jnp.where(first, outs[0], outs[1])
    high = jnp.where(first, outs[1], outs[0])
    left = lax.broadcasted_iota(jnp.int32, low.shape, 1) < 64
    stat = jnp.where(left == first, stats[0], stats[1])
    whole = jnp.concatenate([low, high, stat], axis=1)
    for g in range(out_ref.shape[0]):
        out_ref[token_owner(me, g)] = whole[g * TURN : (g + 1) * TURN].astype(BF16)


def attend(*arrays):
    n = 2 * NY * NX
    keys = sum(v.shape[0] for v in arrays[4:])
    return pl.pallas_call(
        attend_kernel,
        in_specs=[VMEM] * len(arrays),
        out_specs=VMEM,
        out_shape=jax.ShapeDtypeStruct((n, TURN, 3 * HD), BF16),
        compiler_params=limit(12),
        cost_estimate=pl.CostEstimate(
            flops=2 * 2 * 2 * 256 * keys * HD, bytes_accessed=2 * 2**20, transcendentals=2 * 256 * keys
        ),
        name="attend",
    )(*arrays)


def combine_kernel(in_ref, out_ref):
    for j in range(in_ref.shape[0] // 2):
        x = [in_ref[2 * j + i].astype(F32) for i in range(2)]
        for h in range(2):
            at = 2 * HD + 64 * h

            def total(v, i):
                s = at + 24 * i
                return v[:, s : s + 1] + v[:, s + 8 : s + 9] + v[:, s + 16 : s + 17]

            o0, o1 = [v[:, h * HD : (h + 1) * HD] for v in x]
            m0, m1 = [total(v, 0) for v in x]
            l0, l1 = [total(v, 1) for v in x]
            top = jnp.maximum(m0, m1)
            e0, e1 = jnp.exp(m0 - top), jnp.exp(m1 - top)
            out = (o0 * e0 + o1 * e1) / (l0 * e0 + l1 * e1)
            out_ref[:, (2 * j + h) * HD : (2 * j + h + 1) * HD] = out.astype(BF16)


def combine(parts):
    n, t, _ = parts.shape
    return pl.pallas_call(
        combine_kernel,
        out_shape=jax.ShapeDtypeStruct((t, n * HD), BF16),
        compiler_params=limit(4),
        cost_estimate=pl.CostEstimate(flops=n * t * HD * 8, bytes_accessed=n * t * HD * 14, transcendentals=n * t),
        name="combine",
    )(parts)


def shards(cache_hidden, group_hidden, proj_weight, row_place, cache_len, group_place):
    own = jnp.transpose(proj_weight[:, 0], (1, 0, 2))

    one, two = pack(row_place, cache_len, group_place, cache_hidden, group_hidden)
    own, one, two = lax.optimization_barrier((own, one, two))
    other = send(own, SWAP)
    one_up, one_down = send(one, A_UP), send(one, A_DOWN)
    two_up, two_down = send(two, A_UP), send(two, A_DOWN)
    first = join([one, one_up, one_down, send(one_up, A_UP)])
    second = join([two, two_up, two_down, send(two_down, A_DOWN)])
    first_up, second_down = send(first, B_UP), send(second, B_DOWN)
    second_up, first_down = send(second, B_UP), send(first, B_DOWN)
    kv_near = cache_project((first, second), own, other)
    first_up, second_down, kv_near = lax.optimization_barrier((first_up, second_down, kv_near))
    far = send(first_up, B_UP), send(second_down, B_DOWN)

    mid = (first_up, second_up, first_down, second_down)
    kv_mid = cache_project(mid, own, other)
    q_most, kv_most = turn_project((first, second, *mid), own, other)
    *far, kv_mid, q_most = lax.optimization_barrier((*far, kv_mid, q_most))
    q_last, kv_last = turn_project(far, own, other)
    kv_far = cache_project(far, own, other)
    queries = q_most, q_last, send(q_most, SWAP), send(q_last, SWAP)
    parts = attend(*queries, kv_most, kv_last, kv_near, kv_mid, kv_far)
    landed = lax.all_to_all(parts, "seq", split_axis=0, concat_axis=0, tiled=True)
    return combine(landed)


def solution(mesh):
    in_specs = (
        P(("grp", "seq"), None),
        P(("grp", "seq"), None),
        P(None, "seq", None, None),
        P(("grp", "seq")),
        P("grp"),
        P(("grp", "seq")),
    )
    out_specs = P(("grp", "seq"), None)
    return jax.shard_map(shards, mesh=mesh, in_specs=in_specs, out_specs=out_specs, check_vma=False)
```

```python
import functools

import jax
import jax.numpy as jnp
from jax import lax
from jax.experimental import pallas as pl
from jax.experimental.pallas import tpu as pltpu
from jax.sharding import PartitionSpec as P

MASKED_SCORE = -1e30
NY, NX = 4, 4
LIVE = 48
HD = 128
TURN = 8
PART = 20
REST = LIVE - PART
BF16 = jnp.bfloat16
F32 = jnp.float32


def index_of(y, x, c):
    return (y % NY * NX + x % NX) * 2 + c


def ring_pairs(step, first):
    pairs = []
    for y in range(NY):
        for x in range(NX):
            for c in range(2):
                along_x = (c == 0) == first
                dy, dx = (0, step) if along_x else (step, 0)
                pairs.append((index_of(y, x, c), index_of(y + dy, x + dx, c)))
    return pairs


A_UP, A_DOWN = ring_pairs(1, True), ring_pairs(-1, True)
B_UP, B_DOWN = ring_pairs(1, False), ring_pairs(-1, False)
SWAP = [(i, i ^ 1) for i in range(2 * NY * NX)]
OFFSETS = (0, -1, 1, -2)


def token_owner(me, group):
    core = lax.rem(me, 2)
    y, x = lax.div(me, 2 * NX), lax.rem(lax.div(me, 2), NX)
    along_x = core == 0
    if group >= NX * NY:
        core, along_x = 1 - core, core == 1
    b, a = OFFSETS[group % (NX * NY) // 4], OFFSETS[group % 4]
    dy, dx = jnp.where(along_x, b, a), jnp.where(along_x, a, b)
    return (lax.rem(y + dy + NY, NY) * NX + lax.rem(x + dx + NX, NX)) * 2 + core


def send(value, pairs):
    return lax.ppermute(value, "seq", pairs)


VMEM = pl.BlockSpec(memory_space=pltpu.VMEM)


def limit(mib):
    return pltpu.CompilerParams(vmem_limit_bytes=mib * 2**20)


def pack_kernel(*refs):
    sources, (one_ref, two_ref, both_ref), scratch, sems = refs[:5], refs[5:8], refs[8:13], refs[13]
    copies = [pltpu.make_async_copy(a, b, sems.at[i]) for i, (a, b) in enumerate(zip(sources, scratch))]
    for copy in copies:
        copy.start()
    for copy in copies:
        copy.wait()
    place_ref, len_ref, turn_place_ref, rows_ref, turn_ref = scratch
    n, d = rows_ref.shape
    i0 = lax.broadcasted_iota(jnp.int32, (n, n), 0)
    i1 = lax.broadcasted_iota(jnp.int32, (n, n), 1)
    place_col = jnp.sum(jnp.where(i0 == i1, place_ref[...], 0), axis=1, keepdims=True)
    owner = place_col // n
    inner = place_col - owner * n
    o1 = lax.broadcasted_iota(jnp.int32, (n, len_ref.shape[1]), 1)
    length = jnp.sum(jnp.where(o1 == owner, len_ref[...], 0), axis=1, keepdims=True)
    live_col = (inner < length).astype(jnp.int32)
    live_row = jnp.sum(jnp.where(i0 == i1, live_col, 0), axis=0, keepdims=True)
    rank_row = jnp.sum(jnp.where(i0 < i1, live_col, 0), axis=0, keepdims=True)
    rank_row = jnp.where(live_row > 0, rank_row, -1)
    k0 = lax.broadcasted_iota(jnp.int32, (LIVE, n), 0)
    pick = jnp.where(k0 == rank_row, 1.0, 0.0).astype(BF16)
    live = jnp.dot(pick, rows_ref[...], preferred_element_type=F32)
    two_ref[...] = live[PART:].astype(BF16)
    rows = jnp.concatenate([turn_ref[...].astype(F32), live], axis=0).astype(BF16)
    m = TURN + PART
    one_ref[:, :d] = rows[:m]
    both_ref[:, :d] = rows
    t0 = lax.broadcasted_iota(jnp.int32, (TURN + LIVE, TURN), 0)
    t1 = lax.broadcasted_iota(jnp.int32, (TURN + LIVE, TURN), 1)
    turn_col = jnp.sum(jnp.where(t0 == t1, turn_place_ref[...], 0), axis=1, keepdims=True)
    places = jnp.broadcast_to(turn_col.astype(F32), (TURN + LIVE, HD)).astype(BF16)
    one_ref[:, d:] = places[:m]
    both_ref[:, d:] = places


def pack(row_place, cache_len, group_place, cache_hidden, group_hidden):
    n, d = cache_hidden.shape
    m = TURN + PART
    args = (row_place.reshape(1, n), cache_len.reshape(1, -1), group_place.reshape(1, -1), cache_hidden, group_hidden)
    return pl.pallas_call(
        pack_kernel,
        in_specs=[pl.BlockSpec(memory_space=pl.ANY)] * 5,
        out_specs=[VMEM] * 3,
        out_shape=[jax.ShapeDtypeStruct(s, BF16) for s in ((m, d + HD), (REST, d), (m + REST, d + HD))],
        scratch_shapes=[pltpu.VMEM(v.shape, v.dtype) for v in args] + [pltpu.SemaphoreType.DMA((5,))],
        compiler_params=limit(56),
        cost_estimate=pl.CostEstimate(flops=2 * n * LIVE * d, bytes_accessed=4 * n * d, transcendentals=0),
        name="pack_live",
    )(*args)


def stage_kernel(in_ref, out_ref):
    out_ref[...] = in_ref[...]


def stage(x):
    return pl.pallas_call(
        stage_kernel,
        in_specs=[VMEM],
        out_specs=VMEM,
        out_shape=jax.ShapeDtypeStruct(x.shape, x.dtype),
        compiler_params=limit(8),
        cost_estimate=pl.CostEstimate(flops=0, bytes_accessed=4 * x.size, transcendentals=0),
        name="stage_rows",
    )(x)


def join_kernel(turns, own, up, down, far, out_ref):
    m, w = up.shape
    half = slice(0, m) if turns else slice(own.shape[0] - m, own.shape[0])
    x = [own[...].astype(F32)[half, :w], up[...].astype(F32), down[...].astype(F32)[half, :w], far[...].astype(F32)]
    n = len(x) * turns
    if turns:
        out_ref[:n] = jnp.concatenate([v[:turns] for v in x], axis=0).astype(BF16)
    out_ref[n:] = jnp.concatenate([v[turns:] for v in x], axis=0).astype(BF16)


def join(turns, *parts):
    m, w = parts[1].shape
    n = len(parts) * m
    return pl.pallas_call(
        functools.partial(join_kernel, turns),
        in_specs=[VMEM] * len(parts),
        out_specs=VMEM,
        out_shape=jax.ShapeDtypeStruct((n, w), BF16),
        compiler_params=limit(8),
        cost_estimate=pl.CostEstimate(flops=0, bytes_accessed=4 * n * w, transcendentals=0),
        name="join_shards",
    )(*parts)


def split_kernel(in_ref, turn_ref, rows_ref):
    n = turn_ref.shape[0]
    turn_ref[...] = in_ref[:n]
    rows_ref[...] = in_ref[n:, : rows_ref.shape[1]]


def split(block):
    m, w = block.shape
    n = 4 * TURN
    return pl.pallas_call(
        split_kernel,
        in_specs=[VMEM],
        out_specs=[VMEM] * 2,
        out_shape=[jax.ShapeDtypeStruct((n, w), BF16), jax.ShapeDtypeStruct((m - n, w - HD), BF16)],
        compiler_params=limit(8),
        cost_estimate=pl.CostEstimate(flops=0, bytes_accessed=4 * m * w, transcendentals=0),
        name="split_block",
    )(block)


def project_rows(refs, own_ref, other_ref):
    d = own_ref.shape[1]
    x = [r[4 * TURN :, :d] if r.shape[1] > d else r[...] for r in refs]
    w = jnp.concatenate([own_ref[1], own_ref[2], other_ref[1], other_ref[2]], axis=1)
    return jnp.dot(jnp.concatenate(x, axis=0), w, preferred_element_type=F32).astype(BF16)


def turn_kernel(*refs):
    *blocks, own_ref, other_ref, q_ref, kv_ref = refs
    d = own_ref.shape[1]
    turns = jnp.concatenate([r[: 4 * TURN] for r in blocks], axis=0)
    x = turns[:, :d]
    wq = jnp.concatenate([own_ref[0], other_ref[0]], axis=1)
    q_ref[:, : 2 * HD] = jnp.dot(x, wq, preferred_element_type=F32).astype(BF16)
    q_ref[:, 2 * HD :] = turns[:, d:]
    w = jnp.concatenate([own_ref[1], own_ref[2], other_ref[1], other_ref[2]], axis=1)
    kv_ref[...] = jnp.dot(x, w, preferred_element_type=F32).astype(BF16)


def turn_project(blocks, own, other):
    m, d = 16 * TURN, own.shape[1]
    return pl.pallas_call(
        turn_kernel,
        in_specs=[VMEM] * (len(blocks) + 2),
        out_specs=[VMEM] * 2,
        out_shape=[jax.ShapeDtypeStruct((m, 3 * HD), BF16), jax.ShapeDtypeStruct((m, 4 * HD), BF16)],
        compiler_params=limit(16),
        cost_estimate=pl.CostEstimate(flops=2 * m * d * 6 * HD * 6, bytes_accessed=2**20, transcendentals=0),
        name="project_turn",
    )(*blocks, own, other)


def cache_kernel(*refs):
    *rows, own_ref, other_ref, kv_ref = refs
    kv_ref[...] = project_rows(rows, own_ref, other_ref)


def cache_project(rows, own, other):
    m, d = 2 * LIVE * len(rows), own.shape[1]
    return pl.pallas_call(
        cache_kernel,
        in_specs=[VMEM] * (len(rows) + 2),
        out_specs=VMEM,
        out_shape=jax.ShapeDtypeStruct((m, 4 * HD), BF16),
        compiler_params=limit(16),
        cost_estimate=pl.CostEstimate(flops=2 * m * d * 4 * HD, bytes_accessed=2**20, transcendentals=0),
        name="project_cache",
    )(*rows, own, other)


def terms(x):
    hi = x.astype(BF16).astype(F32)
    mid = (x - hi).astype(BF16).astype(F32)
    return [hi, mid, x - hi - mid]


def scores_of(mine, theirs, h, keys):
    q = jnp.concatenate([mine[:, h * HD : (h + 1) * HD], theirs[:, (1 - h) * HD : (2 - h) * HD]], axis=0)
    nt = (((1,), (1,)), ((), ()))
    return lax.dot_general(q, keys, nt, preferred_element_type=F32) * HD ** (-0.5)


def key_value(block, h):
    return block[:, 2 * h * HD : (2 * h + 1) * HD], block[:, (2 * h + 1) * HD : (2 * h + 2) * HD]


def begin_kernel(q_ref, qs_ref, kvf_ref, *refs):
    *cache, sum_ref, top_ref, total_ref = refs
    mine, theirs, fresh = q_ref[...], qs_ref[...], kvf_ref[...]
    q_place = jnp.concatenate([mine[:, 2 * HD :], theirs[:, 2 * HD :]], axis=0).astype(F32)
    k_place = mine[:, 2 * HD :].astype(F32).T[0:1, :]
    seen = k_place <= q_place[:, 0:1]
    for h in range(2):
        pairs = [key_value(r[...], h) for r in cache] + [key_value(fresh, h)]
        s = [scores_of(mine, theirs, h, k) for k, _ in pairs]
        s[-1] = jnp.where(seen, s[-1], MASKED_SCORE)
        top = functools.reduce(jnp.maximum, [jnp.max(t, axis=1, keepdims=True) for t in s])
        total = jnp.zeros_like(top)
        summed = jnp.zeros((top.shape[0], HD), F32)
        for t, (_, v) in zip(s, pairs):
            e = jnp.exp(t - top)
            total += jnp.sum(e, axis=1, keepdims=True)
            summed += jnp.dot(e.astype(BF16), v, preferred_element_type=F32)
        sum_ref[h] = summed
        top_ref[h] = jnp.broadcast_to(top, summed.shape)
        total_ref[h] = jnp.broadcast_to(total, summed.shape)


def begin_attention(*arrays):
    tokens, keys = 2 * arrays[0].shape[0], sum(v.shape[0] for v in arrays[2:])
    return pl.pallas_call(
        begin_kernel,
        in_specs=[VMEM] * len(arrays),
        out_specs=[VMEM] * 3,
        out_shape=[jax.ShapeDtypeStruct((2, tokens, HD), F32)] * 3,
        compiler_params=limit(12),
        cost_estimate=pl.CostEstimate(
            flops=8 * tokens * keys * HD, bytes_accessed=2 * 2**20, transcendentals=2 * tokens * keys
        ),
        name="attend_begin",
    )(*arrays)


def end_kernel(q_ref, qs_ref, sum_ref, top_ref, total_ref, *refs):
    *rows, own_ref, other_ref, out_ref = refs
    me = lax.axis_index("seq")
    first = lax.rem(me, 2) == 0
    kv = project_rows(rows, own_ref, other_ref)
    mine, theirs = q_ref[...], qs_ref[...]
    tokens = sum_ref.shape[1]
    lane = lax.broadcasted_iota(jnp.int32, (tokens, HD), 1)
    outs, stats = [], []
    for h in range(2):
        keys, values = key_value(kv, h)
        s = scores_of(mine, theirs, h, keys)
        old = top_ref[h]
        top = jnp.maximum(old, jnp.max(s, axis=1, keepdims=True))
        e = jnp.exp(s - top[:, 0:1])
        scale = jnp.exp(old - top)
        total = total_ref[h] * scale + jnp.sum(e, axis=1, keepdims=True)
        outs.append(sum_ref[h] * scale + jnp.dot(e.astype(BF16), values, preferred_element_type=F32))
        stat = jnp.zeros((tokens, HD), F32)
        for i, v in enumerate(terms(top) + terms(total)):
            stat = jnp.where(lane % 64 // 8 == i, v, stat)
        stats.append(stat)
    low = jnp.where(first, outs[0], outs[1])
    high = jnp.where(first, outs[1], outs[0])
    stat = jnp.where((lane < 64) == first, stats[0], stats[1])
    whole = jnp.concatenate([low, high, stat], axis=1)
    for g in range(out_ref.shape[0]):
        out_ref[token_owner(me, g)] = whole[g * TURN : (g + 1) * TURN].astype(BF16)


def end_attention(*arrays):
    tokens, d, keys = 2 * arrays[0].shape[0], arrays[-1].shape[1], 4 * LIVE
    return pl.pallas_call(
        end_kernel,
        in_specs=[VMEM] * len(arrays),
        out_specs=VMEM,
        out_shape=jax.ShapeDtypeStruct((2 * NY * NX, TURN, 3 * HD), BF16),
        compiler_params=limit(16),
        cost_estimate=pl.CostEstimate(
            flops=8 * keys * HD * (d + tokens), bytes_accessed=2 * 2**20, transcendentals=2 * tokens * keys
        ),
        name="attend_end",
    )(*arrays)


def combine_kernel(in_ref, out_ref):
    for j in range(in_ref.shape[0] // 2):
        x = [in_ref[2 * j + i].astype(F32) for i in range(2)]
        for h in range(2):
            at = 2 * HD + 64 * h

            def total(v, i):
                s = at + 24 * i
                return v[:, s : s + 1] + v[:, s + 8 : s + 9] + v[:, s + 16 : s + 17]

            o0, o1 = [v[:, h * HD : (h + 1) * HD] for v in x]
            m0, m1 = [total(v, 0) for v in x]
            l0, l1 = [total(v, 1) for v in x]
            top = jnp.maximum(m0, m1)
            e0, e1 = jnp.exp(m0 - top), jnp.exp(m1 - top)
            out = (o0 * e0 + o1 * e1) / (l0 * e0 + l1 * e1)
            out_ref[:, (2 * j + h) * HD : (2 * j + h + 1) * HD] = out.astype(BF16)


def combine(parts):
    n, t, _ = parts.shape
    return pl.pallas_call(
        combine_kernel,
        out_shape=jax.ShapeDtypeStruct((t, n * HD), BF16),
        compiler_params=limit(4),
        cost_estimate=pl.CostEstimate(flops=n * t * HD * 8, bytes_accessed=n * t * HD * 14, transcendentals=n * t),
        name="combine",
    )(parts)


def shards(cache_hidden, group_hidden, proj_weight, row_place, cache_len, group_place):
    own = jnp.transpose(proj_weight[:, 0], (1, 0, 2))

    tie = lax.optimization_barrier
    one, two, both = pack(row_place, cache_len, group_place, cache_hidden, group_hidden)
    own, one, two, both = tie((own, one, two, both))
    one_up, two_up, down = send(one, A_UP), send(two, A_UP), send(both, A_DOWN)
    other = send(own, SWAP)
    one_up, staged = tie((one_up, stage(both)))
    first = join(TURN, staged, one_up, down, send(one_up, A_UP))
    second = join(0, staged, two_up, down, send(two_up, A_UP))
    first_down, second_up = send(first, B_DOWN), send(second, B_UP)
    second_down, first_up = send(second, B_DOWN), send(first, B_UP)
    first_down, second_up, other = tie((first_down, second_up, other))
    turn, rows = split(first_down)
    turn_far = send(turn, B_DOWN)
    far = send(rows, B_DOWN), send(second_up, B_UP)

    q, kv_turn = turn_project((first, first_up, first_down, turn_far), own, other)
    swapped = send(q, SWAP)
    kv = cache_project((first, second, first_up, second_up, first_down, second_down), own, other)
    begun = begin_attention(q, swapped, kv_turn, kv)
    *far, begun = tie((*far, begun))
    parts = end_attention(q, swapped, *begun, *far, own, other)
    landed = lax.all_to_all(parts, "seq", split_axis=0, concat_axis=0, tiled=True)
    return combine(landed)


def solution(mesh):
    in_specs = (
        P(("grp", "seq"), None),
        P(("grp", "seq"), None),
        P(None, "seq", None, None),
        P(("grp", "seq")),
        P("grp"),
        P(("grp", "seq")),
    )
    out_specs = P(("grp", "seq"), None)
    return jax.shard_map(shards, mesh=mesh, in_specs=in_specs, out_specs=out_specs, check_vma=False)
```

```python
import functools

import jax
import jax.numpy as jnp
from jax import lax
from jax.experimental import pallas as pl
from jax.experimental.pallas import tpu as pltpu
from jax.sharding import PartitionSpec as P

MASKED_SCORE = -1e30
NY, NX = 4, 4
LIVE = 48
HD = 128
TURN = 8
PART = 22
REST = LIVE - PART
BF16 = jnp.bfloat16
F32 = jnp.float32


def index_of(y, x, c):
    return (y % NY * NX + x % NX) * 2 + c


def ring_pairs(step, first):
    pairs = []
    for y in range(NY):
        for x in range(NX):
            for c in range(2):
                along_x = (c == 0) == first
                dy, dx = (0, step) if along_x else (step, 0)
                pairs.append((index_of(y, x, c), index_of(y + dy, x + dx, c)))
    return pairs


A_UP, A_DOWN = ring_pairs(1, True), ring_pairs(-1, True)
B_UP, B_DOWN = ring_pairs(1, False), ring_pairs(-1, False)
SWAP = [(i, i ^ 1) for i in range(2 * NY * NX)]
OFFSETS = (0, -1, 1, -2)


def token_owner(me, group):
    core = lax.rem(me, 2)
    y, x = lax.div(me, 2 * NX), lax.rem(lax.div(me, 2), NX)
    along_x = core == 0
    if group >= NX * NY:
        core, along_x = 1 - core, core == 1
    b, a = OFFSETS[group % (NX * NY) // 4], OFFSETS[group % 4]
    dy, dx = jnp.where(along_x, b, a), jnp.where(along_x, a, b)
    return (lax.rem(y + dy + NY, NY) * NX + lax.rem(x + dx + NX, NX)) * 2 + core


def send(value, pairs):
    return lax.ppermute(value, "seq", pairs)


VMEM = pl.BlockSpec(memory_space=pltpu.VMEM)


def limit(mib):
    return pltpu.CompilerParams(vmem_limit_bytes=mib * 2**20)


def pack_kernel(*refs):
    sources, (one_ref, two_ref, both_ref), scratch, sems = refs[:5], refs[5:8], refs[8:13], refs[13]
    copies = [pltpu.make_async_copy(a, b, sems.at[i]) for i, (a, b) in enumerate(zip(sources, scratch))]
    for copy in copies:
        copy.start()
    for copy in copies:
        copy.wait()
    place_ref, len_ref, turn_place_ref, rows_ref, turn_ref = scratch
    n, d = rows_ref.shape
    i0 = lax.broadcasted_iota(jnp.int32, (n, n), 0)
    i1 = lax.broadcasted_iota(jnp.int32, (n, n), 1)
    place_col = jnp.sum(jnp.where(i0 == i1, place_ref[...], 0), axis=1, keepdims=True)
    owner = place_col // n
    inner = place_col - owner * n
    o1 = lax.broadcasted_iota(jnp.int32, (n, len_ref.shape[1]), 1)
    length = jnp.sum(jnp.where(o1 == owner, len_ref[...], 0), axis=1, keepdims=True)
    live_col = (inner < length).astype(jnp.int32)
    live_row = jnp.sum(jnp.where(i0 == i1, live_col, 0), axis=0, keepdims=True)
    rank_row = jnp.sum(jnp.where(i0 < i1, live_col, 0), axis=0, keepdims=True)
    rank_row = jnp.where(live_row > 0, rank_row, -1)
    k0 = lax.broadcasted_iota(jnp.int32, (LIVE, n), 0)
    pick = jnp.where(k0 == rank_row, 1.0, 0.0).astype(BF16)
    live = jnp.dot(pick, rows_ref[...], preferred_element_type=F32)
    two_ref[...] = live[PART:].astype(BF16)
    rows = jnp.concatenate([turn_ref[...].astype(F32), live], axis=0).astype(BF16)
    m = TURN + PART
    one_ref[:, :d] = rows[:m]
    both_ref[:, :d] = rows
    t0 = lax.broadcasted_iota(jnp.int32, (TURN + LIVE, TURN), 0)
    t1 = lax.broadcasted_iota(jnp.int32, (TURN + LIVE, TURN), 1)
    turn_col = jnp.sum(jnp.where(t0 == t1, turn_place_ref[...], 0), axis=1, keepdims=True)
    places = jnp.broadcast_to(turn_col.astype(F32), (TURN + LIVE, HD)).astype(BF16)
    one_ref[:, d:] = places[:m]
    both_ref[:, d:] = places


def pack(row_place, cache_len, group_place, cache_hidden, group_hidden):
    n, d = cache_hidden.shape
    m = TURN + PART
    args = (row_place.reshape(1, n), cache_len.reshape(1, -1), group_place.reshape(1, -1), cache_hidden, group_hidden)
    return pl.pallas_call(
        pack_kernel,
        in_specs=[pl.BlockSpec(memory_space=pl.ANY)] * 5,
        out_specs=[VMEM] * 3,
        out_shape=[jax.ShapeDtypeStruct(s, BF16) for s in ((m, d + HD), (REST, d), (m + REST, d + HD))],
        scratch_shapes=[pltpu.VMEM(v.shape, v.dtype) for v in args] + [pltpu.SemaphoreType.DMA((5,))],
        compiler_params=limit(56),
        cost_estimate=pl.CostEstimate(flops=2 * n * LIVE * d, bytes_accessed=4 * n * d, transcendentals=0),
        name="pack_live",
    )(*args)


def stage_kernel(in_ref, out_ref):
    out_ref[...] = in_ref[...]


def stage(x):
    return pl.pallas_call(
        stage_kernel,
        in_specs=[VMEM],
        out_specs=VMEM,
        out_shape=jax.ShapeDtypeStruct(x.shape, x.dtype),
        compiler_params=limit(8),
        cost_estimate=pl.CostEstimate(flops=0, bytes_accessed=4 * x.size, transcendentals=0),
        name="stage_rows",
    )(x)


def join_kernel(turns, own, up, down, far, out_ref):
    m, w = up.shape
    half = slice(0, m) if turns else slice(own.shape[0] - m, own.shape[0])
    x = [own[...].astype(F32)[half, :w], up[...].astype(F32), down[...].astype(F32)[half, :w], far[...].astype(F32)]
    n = len(x) * turns
    if turns:
        out_ref[:n] = jnp.concatenate([v[:turns] for v in x], axis=0).astype(BF16)
    out_ref[n:] = jnp.concatenate([v[turns:] for v in x], axis=0).astype(BF16)


def join(turns, *parts):
    m, w = parts[1].shape
    n = len(parts) * m
    return pl.pallas_call(
        functools.partial(join_kernel, turns),
        in_specs=[VMEM] * len(parts),
        out_specs=VMEM,
        out_shape=jax.ShapeDtypeStruct((n, w), BF16),
        compiler_params=limit(8),
        cost_estimate=pl.CostEstimate(flops=0, bytes_accessed=4 * n * w, transcendentals=0),
        name="join_shards",
    )(*parts)


def split_kernel(in_ref, turn_ref, rows_ref):
    n = turn_ref.shape[0]
    turn_ref[...] = in_ref[:n]
    rows_ref[...] = in_ref[n:, : rows_ref.shape[1]]


def split(block):
    m, w = block.shape
    n = 4 * TURN
    return pl.pallas_call(
        split_kernel,
        in_specs=[VMEM],
        out_specs=[VMEM] * 2,
        out_shape=[jax.ShapeDtypeStruct((n, w), BF16), jax.ShapeDtypeStruct((m - n, w - HD), BF16)],
        compiler_params=limit(8),
        cost_estimate=pl.CostEstimate(flops=0, bytes_accessed=4 * m * w, transcendentals=0),
        name="split_block",
    )(block)


def project_rows(refs, own_ref, other_ref):
    d = own_ref.shape[1]
    x = [r[4 * TURN :, :d] if r.shape[1] > d else r[...] for r in refs]
    w = jnp.concatenate([own_ref[1], own_ref[2], other_ref[1], other_ref[2]], axis=1)
    return jnp.dot(jnp.concatenate(x, axis=0), w, preferred_element_type=F32).astype(BF16)


def turn_kernel(*refs):
    *blocks, own_ref, other_ref, q_ref, kv_ref = refs
    d = own_ref.shape[1]
    turns = jnp.concatenate([r[: 4 * TURN] for r in blocks], axis=0)
    x = turns[:, :d]
    wq = jnp.concatenate([own_ref[0], other_ref[0]], axis=1)
    q_ref[:, : 2 * HD] = jnp.dot(x, wq, preferred_element_type=F32).astype(BF16)
    q_ref[:, 2 * HD :] = turns[:, d:]
    w = jnp.concatenate([own_ref[1], own_ref[2], other_ref[1], other_ref[2]], axis=1)
    kv_ref[...] = jnp.dot(x, w, preferred_element_type=F32).astype(BF16)


def turn_project(blocks, own, other):
    m, d = 16 * TURN, own.shape[1]
    return pl.pallas_call(
        turn_kernel,
        in_specs=[VMEM] * (len(blocks) + 2),
        out_specs=[VMEM] * 2,
        out_shape=[jax.ShapeDtypeStruct((m, 3 * HD), BF16), jax.ShapeDtypeStruct((m, 4 * HD), BF16)],
        compiler_params=limit(16),
        cost_estimate=pl.CostEstimate(flops=2 * m * d * 6 * HD * 6, bytes_accessed=2**20, transcendentals=0),
        name="project_turn",
    )(*blocks, own, other)


def cache_kernel(*refs):
    *rows, own_ref, other_ref, kv_ref = refs
    kv_ref[...] = project_rows(rows, own_ref, other_ref)


def cache_project(rows, own, other):
    m, d = 2 * LIVE * len(rows), own.shape[1]
    return pl.pallas_call(
        cache_kernel,
        in_specs=[VMEM] * (len(rows) + 2),
        out_specs=VMEM,
        out_shape=jax.ShapeDtypeStruct((m, 4 * HD), BF16),
        compiler_params=limit(16),
        cost_estimate=pl.CostEstimate(flops=2 * m * d * 4 * HD, bytes_accessed=2**20, transcendentals=0),
        name="project_cache",
    )(*rows, own, other)


def terms(x):
    hi = x.astype(BF16).astype(F32)
    mid = (x - hi).astype(BF16).astype(F32)
    return [hi, mid, x - hi - mid]


def scores_of(mine, theirs, h, keys):
    q = jnp.concatenate([mine[:, h * HD : (h + 1) * HD], theirs[:, (1 - h) * HD : (2 - h) * HD]], axis=0)
    nt = (((1,), (1,)), ((), ()))
    return lax.dot_general(q, keys, nt, preferred_element_type=F32) * HD ** (-0.5)


def key_value(block, h):
    return block[:, 2 * h * HD : (2 * h + 1) * HD], block[:, (2 * h + 1) * HD : (2 * h + 2) * HD]


def begin_kernel(q_ref, qs_ref, kvf_ref, *refs):
    *cache, sum_ref, top_ref, total_ref = refs
    mine, theirs, fresh = q_ref[...], qs_ref[...], kvf_ref[...]
    q_place = jnp.concatenate([mine[:, 2 * HD :], theirs[:, 2 * HD :]], axis=0).astype(F32)
    k_place = mine[:, 2 * HD :].astype(F32).T[0:1, :]
    seen = k_place <= q_place[:, 0:1]
    for h in range(2):
        pairs = [key_value(r[...], h) for r in cache] + [key_value(fresh, h)]
        s = [scores_of(mine, theirs, h, k) for k, _ in pairs]
        s[-1] = jnp.where(seen, s[-1], MASKED_SCORE)
        top = functools.reduce(jnp.maximum, [jnp.max(t, axis=1, keepdims=True) for t in s])
        total = jnp.zeros_like(top)
        summed = jnp.zeros((top.shape[0], HD), F32)
        for t, (_, v) in zip(s, pairs):
            e = jnp.exp(t - top)
            total += jnp.sum(e, axis=1, keepdims=True)
            summed += jnp.dot(e.astype(BF16), v, preferred_element_type=F32)
        sum_ref[h] = summed
        top_ref[h] = jnp.broadcast_to(top, summed.shape)
        total_ref[h] = jnp.broadcast_to(total, summed.shape)


def begin_attention(*arrays):
    tokens, keys = 2 * arrays[0].shape[0], sum(v.shape[0] for v in arrays[2:])
    return pl.pallas_call(
        begin_kernel,
        in_specs=[VMEM] * len(arrays),
        out_specs=[VMEM] * 3,
        out_shape=[jax.ShapeDtypeStruct((2, tokens, HD), F32)] * 3,
        compiler_params=limit(12),
        cost_estimate=pl.CostEstimate(
            flops=8 * tokens * keys * HD, bytes_accessed=2 * 2**20, transcendentals=2 * tokens * keys
        ),
        name="attend_begin",
    )(*arrays)


def end_kernel(q_ref, qs_ref, sum_ref, top_ref, total_ref, *refs):
    *rows, own_ref, other_ref, out_ref = refs
    me = lax.axis_index("seq")
    first = lax.rem(me, 2) == 0
    kv = project_rows(rows, own_ref, other_ref)
    mine, theirs = q_ref[...], qs_ref[...]
    tokens = sum_ref.shape[1]
    lane = lax.broadcasted_iota(jnp.int32, (tokens, HD), 1)
    outs, stats = [], []
    for h in range(2):
        keys, values = key_value(kv, h)
        s = scores_of(mine, theirs, h, keys)
        old = top_ref[h]
        top = jnp.maximum(old, jnp.max(s, axis=1, keepdims=True))
        e = jnp.exp(s - top[:, 0:1])
        scale = jnp.exp(old - top)
        total = total_ref[h] * scale + jnp.sum(e, axis=1, keepdims=True)
        outs.append(sum_ref[h] * scale + jnp.dot(e.astype(BF16), values, preferred_element_type=F32))
        stat = jnp.zeros((tokens, HD), F32)
        for i, v in enumerate(terms(top) + terms(total)):
            stat = jnp.where(lane % 64 // 8 == i, v, stat)
        stats.append(stat)
    low = jnp.where(first, outs[0], outs[1])
    high = jnp.where(first, outs[1], outs[0])
    stat = jnp.where((lane < 64) == first, stats[0], stats[1])
    whole = jnp.concatenate([low, high, stat], axis=1)
    for g in range(out_ref.shape[0]):
        out_ref[token_owner(me, g)] = whole[g * TURN : (g + 1) * TURN].astype(BF16)


def end_attention(*arrays):
    tokens, d, keys = 2 * arrays[0].shape[0], arrays[-1].shape[1], 4 * LIVE
    return pl.pallas_call(
        end_kernel,
        in_specs=[VMEM] * len(arrays),
        out_specs=VMEM,
        out_shape=jax.ShapeDtypeStruct((2 * NY * NX, TURN, 3 * HD), BF16),
        compiler_params=limit(16),
        cost_estimate=pl.CostEstimate(
            flops=8 * keys * HD * (d + tokens), bytes_accessed=2 * 2**20, transcendentals=2 * tokens * keys
        ),
        name="attend_end",
    )(*arrays)


def combine_kernel(in_ref, out_ref):
    for j in range(in_ref.shape[0] // 2):
        x = [in_ref[2 * j + i].astype(F32) for i in range(2)]
        stat = [v[:, 2 * HD :] for v in x]
        stat = [v + pltpu.roll(v, HD - 8, 1) + pltpu.roll(v, HD - 16, 1) for v in stat]
        total = [pltpu.roll(v, HD - 24, 1) for v in stat]
        top = jnp.maximum(*stat)
        scale = [jnp.exp(v - top) for v in stat]
        share = 1.0 / (total[0] * scale[0] + total[1] * scale[1])
        scale = [v * share for v in scale]
        for h in range(2):
            cols = slice(h * HD, (h + 1) * HD)
            out = sum(v[:, cols] * e[:, 64 * h : 64 * h + 1] for v, e in zip(x, scale))
            out_ref[:, (2 * j + h) * HD : (2 * j + h + 1) * HD] = out.astype(BF16)


def combine(parts):
    n, t, _ = parts.shape
    return pl.pallas_call(
        combine_kernel,
        out_shape=jax.ShapeDtypeStruct((t, n * HD), BF16),
        compiler_params=limit(4),
        cost_estimate=pl.CostEstimate(flops=n * t * HD * 8, bytes_accessed=n * t * HD * 14, transcendentals=n * t),
        name="combine",
    )(parts)


def shards(cache_hidden, group_hidden, proj_weight, row_place, cache_len, group_place):
    own = jnp.transpose(proj_weight[:, 0], (1, 0, 2))

    tie = lax.optimization_barrier
    one, two, both = pack(row_place, cache_len, group_place, cache_hidden, group_hidden)
    own, one, two, both = tie((own, one, two, both))
    one_up, two_up, down = send(one, A_UP), send(two, A_UP), send(both, A_DOWN)
    other = send(own, SWAP)
    one_up, staged = tie((one_up, stage(both)))
    first = join(TURN, staged, one_up, down, send(one_up, A_UP))
    second = join(0, staged, two_up, down, send(two_up, A_UP))
    first_down, second_up = send(first, B_DOWN), send(second, B_UP)
    second_down, first_up = send(second, B_DOWN), send(first, B_UP)
    first_down, second_up, other = tie((first_down, second_up, other))
    turn, rows = split(first_down)
    turn_far = send(turn, B_DOWN)
    far = send(rows, B_DOWN), send(second_up, B_UP)

    q, kv_turn = turn_project((first, first_up, first_down, turn_far), own, other)
    swapped = send(q, SWAP)
    kv = cache_project((first, second, first_up, second_up, first_down, second_down), own, other)
    begun = begin_attention(q, swapped, kv_turn, kv)
    *far, begun = tie((*far, begun))
    parts = end_attention(q, swapped, *begun, *far, own, other)
    landed = lax.all_to_all(parts, "seq", split_axis=0, concat_axis=0, tiled=True)
    return combine(landed)


def solution(mesh):
    in_specs = (
        P(("grp", "seq"), None),
        P(("grp", "seq"), None),
        P(None, "seq", None, None),
        P(("grp", "seq")),
        P("grp"),
        P(("grp", "seq")),
    )
    out_specs = P(("grp", "seq"), None)
    return jax.shard_map(shards, mesh=mesh, in_specs=in_specs, out_specs=out_specs, check_vma=False)
```

```python
import functools

import jax
import jax.numpy as jnp
from jax import lax
from jax.experimental import pallas as pl
from jax.experimental.pallas import tpu as pltpu
from jax.sharding import PartitionSpec as P

MASKED_SCORE = -1e30
NY, NX = 4, 4
LIVE = 48
HD = 128
TURN = 8
PART = 22
REST = LIVE - PART
BF16 = jnp.bfloat16
F32 = jnp.float32


def index_of(y, x, c):
    return (y % NY * NX + x % NX) * 2 + c


def ring_pairs(step, first):
    pairs = []
    for y in range(NY):
        for x in range(NX):
            for c in range(2):
                along_x = (c == 0) == first
                dy, dx = (0, step) if along_x else (step, 0)
                pairs.append((index_of(y, x, c), index_of(y + dy, x + dx, c)))
    return pairs


A_UP, A_DOWN = ring_pairs(1, True), ring_pairs(-1, True)
B_UP, B_DOWN = ring_pairs(1, False), ring_pairs(-1, False)
SWAP = [(i, i ^ 1) for i in range(2 * NY * NX)]
OFFSETS = (0, -1, 1, -2)


def token_owner(me, group):
    core = lax.rem(me, 2)
    y, x = lax.div(me, 2 * NX), lax.rem(lax.div(me, 2), NX)
    along_x = core == 0
    if group >= NX * NY:
        core, along_x = 1 - core, core == 1
    b, a = OFFSETS[group % (NX * NY) // 4], OFFSETS[group % 4]
    dy, dx = jnp.where(along_x, b, a), jnp.where(along_x, a, b)
    return (lax.rem(y + dy + NY, NY) * NX + lax.rem(x + dx + NX, NX)) * 2 + core


def send(value, pairs):
    return lax.ppermute(value, "seq", pairs)


VMEM = pl.BlockSpec(memory_space=pltpu.VMEM)


def limit(mib):
    return pltpu.CompilerParams(vmem_limit_bytes=mib * 2**20)


def pack_kernel(place_ref, len_ref, turn_place_ref, rows_ref, turn_ref, one_ref, two_ref, both_ref):
    n, d = rows_ref.shape
    i0 = lax.broadcasted_iota(jnp.int32, (n, n), 0)
    i1 = lax.broadcasted_iota(jnp.int32, (n, n), 1)
    place_col = jnp.sum(jnp.where(i0 == i1, place_ref[...], 0), axis=1, keepdims=True)
    owner = place_col // n
    inner = place_col - owner * n
    o1 = lax.broadcasted_iota(jnp.int32, (n, len_ref.shape[1]), 1)
    length = jnp.sum(jnp.where(o1 == owner, len_ref[...], 0), axis=1, keepdims=True)
    live_col = (inner < length).astype(jnp.int32)
    live_row = jnp.sum(jnp.where(i0 == i1, live_col, 0), axis=0, keepdims=True)
    rank_row = jnp.sum(jnp.where(i0 < i1, live_col, 0), axis=0, keepdims=True)
    rank_row = jnp.where(live_row > 0, rank_row, -1)
    k0 = lax.broadcasted_iota(jnp.int32, (LIVE, n), 0)
    pick = jnp.where(k0 == rank_row, 1.0, 0.0).astype(BF16)
    live = jnp.dot(pick, rows_ref[...], preferred_element_type=F32)
    two_ref[...] = live[PART:].astype(BF16)
    rows = jnp.concatenate([turn_ref[...].astype(F32), live], axis=0).astype(BF16)
    m = TURN + PART
    one_ref[:, :d] = rows[:m]
    both_ref[:, :d] = rows
    t0 = lax.broadcasted_iota(jnp.int32, (TURN + LIVE, TURN), 0)
    t1 = lax.broadcasted_iota(jnp.int32, (TURN + LIVE, TURN), 1)
    turn_col = jnp.sum(jnp.where(t0 == t1, turn_place_ref[...], 0), axis=1, keepdims=True)
    places = jnp.broadcast_to(turn_col.astype(F32), (TURN + LIVE, HD)).astype(BF16)
    one_ref[:, d:] = places[:m]
    both_ref[:, d:] = places


def pack(row_place, cache_len, group_place, cache_hidden, group_hidden):
    n, d = cache_hidden.shape
    m = TURN + PART
    args = (row_place.reshape(1, n), cache_len.reshape(1, -1), group_place.reshape(1, -1), cache_hidden, group_hidden)
    return pl.pallas_call(
        pack_kernel,
        in_specs=[VMEM] * 5,
        out_specs=[VMEM] * 3,
        out_shape=[jax.ShapeDtypeStruct(s, BF16) for s in ((m, d + HD), (REST, d), (m + REST, d + HD))],
        compiler_params=limit(56),
        cost_estimate=pl.CostEstimate(flops=2 * n * LIVE * d, bytes_accessed=4 * n * d, transcendentals=0),
        name="pack_live",
    )(*args)


def stage_kernel(in_ref, out_ref):
    out_ref[...] = in_ref[...]


def stage(x):
    return pl.pallas_call(
        stage_kernel,
        in_specs=[VMEM],
        out_specs=VMEM,
        out_shape=jax.ShapeDtypeStruct(x.shape, x.dtype),
        compiler_params=limit(8),
        cost_estimate=pl.CostEstimate(flops=0, bytes_accessed=4 * x.size, transcendentals=0),
        name="stage_rows",
    )(x)


def join_kernel(turns, own, up, down, far, out_ref):
    m, w = up.shape
    half = slice(0, m) if turns else slice(own.shape[0] - m, own.shape[0])
    x = [own[...].astype(F32)[half, :w], up[...].astype(F32), down[...].astype(F32)[half, :w], far[...].astype(F32)]
    n = len(x) * turns
    if turns:
        out_ref[:n] = jnp.concatenate([v[:turns] for v in x], axis=0).astype(BF16)
    out_ref[n:] = jnp.concatenate([v[turns:] for v in x], axis=0).astype(BF16)


def join(turns, *parts):
    m, w = parts[1].shape
    n = len(parts) * m
    return pl.pallas_call(
        functools.partial(join_kernel, turns),
        in_specs=[VMEM] * len(parts),
        out_specs=VMEM,
        out_shape=jax.ShapeDtypeStruct((n, w), BF16),
        compiler_params=limit(8),
        cost_estimate=pl.CostEstimate(flops=0, bytes_accessed=4 * n * w, transcendentals=0),
        name="join_shards",
    )(*parts)


def split_kernel(in_ref, turn_ref, rows_ref):
    n = turn_ref.shape[0]
    turn_ref[...] = in_ref[:n]
    rows_ref[...] = in_ref[n:, : rows_ref.shape[1]]


def split(block):
    m, w = block.shape
    n = 4 * TURN
    return pl.pallas_call(
        split_kernel,
        in_specs=[VMEM],
        out_specs=[VMEM] * 2,
        out_shape=[jax.ShapeDtypeStruct((n, w), BF16), jax.ShapeDtypeStruct((m - n, w - HD), BF16)],
        compiler_params=limit(8),
        cost_estimate=pl.CostEstimate(flops=0, bytes_accessed=4 * m * w, transcendentals=0),
        name="split_block",
    )(block)


def project_rows(refs, own_ref, other_ref):
    d = own_ref.shape[1]
    x = [r[4 * TURN :, :d] if r.shape[1] > d else r[...] for r in refs]
    w = jnp.concatenate([own_ref[1], own_ref[2], other_ref[1], other_ref[2]], axis=1)
    return jnp.dot(jnp.concatenate(x, axis=0), w, preferred_element_type=F32).astype(BF16)


def turn_kernel(*refs):
    *blocks, own_ref, other_ref, q_ref, kv_ref = refs
    d = own_ref.shape[1]
    turns = jnp.concatenate([r[: 4 * TURN] for r in blocks], axis=0)
    x = turns[:, :d]
    wq = jnp.concatenate([own_ref[0], other_ref[0]], axis=1)
    q_ref[:, : 2 * HD] = jnp.dot(x, wq, preferred_element_type=F32).astype(BF16)
    q_ref[:, 2 * HD :] = turns[:, d:]
    w = jnp.concatenate([own_ref[1], own_ref[2], other_ref[1], other_ref[2]], axis=1)
    kv_ref[...] = jnp.dot(x, w, preferred_element_type=F32).astype(BF16)


def turn_project(blocks, own, other):
    m, d = 16 * TURN, own.shape[1]
    return pl.pallas_call(
        turn_kernel,
        in_specs=[VMEM] * (len(blocks) + 2),
        out_specs=[VMEM] * 2,
        out_shape=[jax.ShapeDtypeStruct((m, 3 * HD), BF16), jax.ShapeDtypeStruct((m, 4 * HD), BF16)],
        compiler_params=limit(16),
        cost_estimate=pl.CostEstimate(flops=2 * m * d * 6 * HD * 6, bytes_accessed=2**20, transcendentals=0),
        name="project_turn",
    )(*blocks, own, other)


def cache_kernel(*refs):
    *rows, own_ref, other_ref, kv_ref = refs
    kv_ref[...] = project_rows(rows, own_ref, other_ref)


def cache_project(rows, own, other):
    m, d = 2 * LIVE * len(rows), own.shape[1]
    return pl.pallas_call(
        cache_kernel,
        in_specs=[VMEM] * (len(rows) + 2),
        out_specs=VMEM,
        out_shape=jax.ShapeDtypeStruct((m, 4 * HD), BF16),
        compiler_params=limit(16),
        cost_estimate=pl.CostEstimate(flops=2 * m * d * 4 * HD, bytes_accessed=2**20, transcendentals=0),
        name="project_cache",
    )(*rows, own, other)


def terms(x):
    hi = x.astype(BF16).astype(F32)
    mid = (x - hi).astype(BF16).astype(F32)
    return [hi, mid, x - hi - mid]


def scores_of(mine, theirs, h, keys):
    q = jnp.concatenate([mine[:, h * HD : (h + 1) * HD], theirs[:, (1 - h) * HD : (2 - h) * HD]], axis=0)
    nt = (((1,), (1,)), ((), ()))
    return lax.dot_general(q, keys, nt, preferred_element_type=F32) * HD ** (-0.5)


def key_value(block, h):
    return block[:, 2 * h * HD : (2 * h + 1) * HD], block[:, (2 * h + 1) * HD : (2 * h + 2) * HD]


def begin_kernel(q_ref, qs_ref, kvf_ref, *refs):
    *cache, sum_ref, top_ref, total_ref = refs
    mine, theirs, fresh = q_ref[...], qs_ref[...], kvf_ref[...]
    q_place = jnp.concatenate([mine[:, 2 * HD :], theirs[:, 2 * HD :]], axis=0).astype(F32)
    k_place = mine[:, 2 * HD :].astype(F32).T[0:1, :]
    seen = k_place <= q_place[:, 0:1]
    for h in range(2):
        pairs = [key_value(r[...], h) for r in cache] + [key_value(fresh, h)]
        s = [scores_of(mine, theirs, h, k) for k, _ in pairs]
        s[-1] = jnp.where(seen, s[-1], MASKED_SCORE)
        top = functools.reduce(jnp.maximum, [jnp.max(t, axis=1, keepdims=True) for t in s])
        total = jnp.zeros_like(top)
        summed = jnp.zeros((top.shape[0], HD), F32)
        for t, (_, v) in zip(s, pairs):
            e = jnp.exp(t - top)
            total += jnp.sum(e, axis=1, keepdims=True)
            summed += jnp.dot(e.astype(BF16), v, preferred_element_type=F32)
        sum_ref[h] = summed
        top_ref[h] = jnp.broadcast_to(top, summed.shape)
        total_ref[h] = jnp.broadcast_to(total, summed.shape)


def begin_attention(*arrays):
    tokens, keys = 2 * arrays[0].shape[0], sum(v.shape[0] for v in arrays[2:])
    return pl.pallas_call(
        begin_kernel,
        in_specs=[VMEM] * len(arrays),
        out_specs=[VMEM] * 3,
        out_shape=[jax.ShapeDtypeStruct((2, tokens, HD), F32)] * 3,
        compiler_params=limit(12),
        cost_estimate=pl.CostEstimate(
            flops=8 * tokens * keys * HD, bytes_accessed=2 * 2**20, transcendentals=2 * tokens * keys
        ),
        name="attend_begin",
    )(*arrays)


def end_kernel(q_ref, qs_ref, sum_ref, top_ref, total_ref, *refs):
    *rows, own_ref, other_ref, out_ref = refs
    me = lax.axis_index("seq")
    first = lax.rem(me, 2) == 0
    kv = project_rows(rows, own_ref, other_ref)
    mine, theirs = q_ref[...], qs_ref[...]
    tokens = sum_ref.shape[1]
    lane = lax.broadcasted_iota(jnp.int32, (tokens, HD), 1)
    outs, stats = [], []
    for h in range(2):
        keys, values = key_value(kv, h)
        s = scores_of(mine, theirs, h, keys)
        old = top_ref[h]
        top = jnp.maximum(old, jnp.max(s, axis=1, keepdims=True))
        e = jnp.exp(s - top[:, 0:1])
        scale = jnp.exp(old - top)
        total = total_ref[h] * scale + jnp.sum(e, axis=1, keepdims=True)
        outs.append(sum_ref[h] * scale + jnp.dot(e.astype(BF16), values, preferred_element_type=F32))
        stat = jnp.zeros((tokens, HD), F32)
        for i, v in enumerate(terms(top) + terms(total)):
            stat = jnp.where(lane % 64 // 8 == i, v, stat)
        stats.append(stat)
    low = jnp.where(first, outs[0], outs[1])
    high = jnp.where(first, outs[1], outs[0])
    stat = jnp.where((lane < 64) == first, stats[0], stats[1])
    whole = jnp.concatenate([low, high, stat], axis=1)
    for g in range(out_ref.shape[0]):
        out_ref[token_owner(me, g)] = whole[g * TURN : (g + 1) * TURN].astype(BF16)


def end_attention(*arrays):
    tokens, d, keys = 2 * arrays[0].shape[0], arrays[-1].shape[1], 4 * LIVE
    return pl.pallas_call(
        end_kernel,
        in_specs=[VMEM] * len(arrays),
        out_specs=VMEM,
        out_shape=jax.ShapeDtypeStruct((2 * NY * NX, TURN, 3 * HD), BF16),
        compiler_params=limit(16),
        cost_estimate=pl.CostEstimate(
            flops=8 * keys * HD * (d + tokens), bytes_accessed=2 * 2**20, transcendentals=2 * tokens * keys
        ),
        name="attend_end",
    )(*arrays)


def combine_kernel(in_ref, out_ref):
    for j in range(in_ref.shape[0] // 2):
        x = [in_ref[2 * j + i].astype(F32) for i in range(2)]
        stat = [v[:, 2 * HD :] for v in x]
        stat = [v + pltpu.roll(v, HD - 8, 1) + pltpu.roll(v, HD - 16, 1) for v in stat]
        total = [pltpu.roll(v, HD - 24, 1) for v in stat]
        top = jnp.maximum(*stat)
        scale = [jnp.exp(v - top) for v in stat]
        share = 1.0 / (total[0] * scale[0] + total[1] * scale[1])
        scale = [v * share for v in scale]
        for h in range(2):
            cols = slice(h * HD, (h + 1) * HD)
            out = sum(v[:, cols] * e[:, 64 * h : 64 * h + 1] for v, e in zip(x, scale))
            out_ref[:, (2 * j + h) * HD : (2 * j + h + 1) * HD] = out.astype(BF16)


def combine(parts):
    n, t, _ = parts.shape
    return pl.pallas_call(
        combine_kernel,
        out_shape=jax.ShapeDtypeStruct((t, n * HD), BF16),
        compiler_params=limit(4),
        cost_estimate=pl.CostEstimate(flops=n * t * HD * 8, bytes_accessed=n * t * HD * 14, transcendentals=n * t),
        name="combine",
    )(parts)


def shards(cache_hidden, group_hidden, proj_weight, row_place, cache_len, group_place):
    own = jnp.transpose(proj_weight[:, 0], (1, 0, 2))

    tie = lax.optimization_barrier
    one, two, both = pack(row_place, cache_len, group_place, cache_hidden, group_hidden)
    own, one, two, both = tie((own, one, two, both))
    one_up, two_up, down = send(one, A_UP), send(two, A_UP), send(both, A_DOWN)
    other = send(own, SWAP)
    one_up, staged = tie((one_up, stage(both)))
    first = join(TURN, staged, one_up, down, send(one_up, A_UP))
    second = join(0, staged, two_up, down, send(two_up, A_UP))
    first_down, second_up = send(first, B_DOWN), send(second, B_UP)
    second_down, first_up = send(second, B_DOWN), send(first, B_UP)
    first_down, second_up, other = tie((first_down, second_up, other))
    turn, rows = split(first_down)
    turn_far = send(turn, B_DOWN)
    far = send(rows, B_DOWN), send(second_up, B_UP)

    q, kv_turn = turn_project((first, first_up, first_down, turn_far), own, other)
    swapped = send(q, SWAP)
    kv = cache_project((first, second, first_up, second_up, first_down, second_down), own, other)
    begun = begin_attention(q, swapped, kv_turn, kv)
    *far, begun = tie((*far, begun))
    parts = end_attention(q, swapped, *begun, *far, own, other)
    landed = lax.all_to_all(parts, "seq", split_axis=0, concat_axis=0, tiled=True)
    return combine(landed)


def solution(mesh):
    in_specs = (
        P(("grp", "seq"), None),
        P(("grp", "seq"), None),
        P(None, "seq", None, None),
        P(("grp", "seq")),
        P("grp"),
        P(("grp", "seq")),
    )
    out_specs = P(("grp", "seq"), None)
    return jax.shard_map(shards, mesh=mesh, in_specs=in_specs, out_specs=out_specs, check_vma=False)
```

```python
import functools

import jax
import jax.numpy as jnp
from jax import lax
from jax.experimental import pallas as pl
from jax.experimental.pallas import tpu as pltpu
from jax.sharding import PartitionSpec as P

MASKED_SCORE = -1e30
NY, NX = 4, 4
LIVE = 48
HD = 128
TURN = 8
PART = 22
REST = LIVE - PART
BF16 = jnp.bfloat16
F32 = jnp.float32


def index_of(y, x, c):
    return (y % NY * NX + x % NX) * 2 + c


def ring_pairs(step, first):
    pairs = []
    for y in range(NY):
        for x in range(NX):
            for c in range(2):
                along_x = (c == 0) == first
                dy, dx = (0, step) if along_x else (step, 0)
                pairs.append((index_of(y, x, c), index_of(y + dy, x + dx, c)))
    return pairs


A_UP, A_DOWN = ring_pairs(1, False), ring_pairs(-1, False)
B_UP, B_DOWN = ring_pairs(1, True), ring_pairs(-1, True)
SWAP = [(i, i ^ 1) for i in range(2 * NY * NX)]
OFFSETS = (0, -1, 1, -2)


def token_owner(me, group):
    core = lax.rem(me, 2)
    y, x = lax.div(me, 2 * NX), lax.rem(lax.div(me, 2), NX)
    along_x = core == 1
    if group >= NX * NY:
        core, along_x = 1 - core, core == 0
    b, a = OFFSETS[group % (NX * NY) // 4], OFFSETS[group % 4]
    dy, dx = jnp.where(along_x, b, a), jnp.where(along_x, a, b)
    return (lax.rem(y + dy + NY, NY) * NX + lax.rem(x + dx + NX, NX)) * 2 + core


def send(value, pairs):
    return lax.ppermute(value, "seq", pairs)


VMEM = pl.BlockSpec(memory_space=pltpu.VMEM)


def limit(mib):
    return pltpu.CompilerParams(vmem_limit_bytes=mib * 2**20)


def pack_kernel(place_ref, len_ref, turn_place_ref, rows_ref, turn_ref, one_ref, two_ref, both_ref):
    n, d = rows_ref.shape
    i0 = lax.broadcasted_iota(jnp.int32, (n, n), 0)
    i1 = lax.broadcasted_iota(jnp.int32, (n, n), 1)
    place_col = jnp.sum(jnp.where(i0 == i1, place_ref[...], 0), axis=1, keepdims=True)
    owner = place_col // n
    inner = place_col - owner * n
    o1 = lax.broadcasted_iota(jnp.int32, (n, len_ref.shape[1]), 1)
    length = jnp.sum(jnp.where(o1 == owner, len_ref[...], 0), axis=1, keepdims=True)
    live_col = (inner < length).astype(jnp.int32)
    live_row = jnp.sum(jnp.where(i0 == i1, live_col, 0), axis=0, keepdims=True)
    rank_row = jnp.sum(jnp.where(i0 < i1, live_col, 0), axis=0, keepdims=True)
    rank_row = jnp.where(live_row > 0, rank_row, -1)
    k0 = lax.broadcasted_iota(jnp.int32, (LIVE, n), 0)
    pick = jnp.where(k0 == rank_row, 1.0, 0.0).astype(BF16)
    live = jnp.dot(pick, rows_ref[...], preferred_element_type=F32)
    two_ref[...] = live[PART:].astype(BF16)
    rows = jnp.concatenate([turn_ref[...].astype(F32), live], axis=0).astype(BF16)
    m = TURN + PART
    one_ref[:, :d] = rows[:m]
    both_ref[:, :d] = rows
    t0 = lax.broadcasted_iota(jnp.int32, (TURN + LIVE, TURN), 0)
    t1 = lax.broadcasted_iota(jnp.int32, (TURN + LIVE, TURN), 1)
    turn_col = jnp.sum(jnp.where(t0 == t1, turn_place_ref[...], 0), axis=1, keepdims=True)
    places = jnp.broadcast_to(turn_col.astype(F32), (TURN + LIVE, HD)).astype(BF16)
    one_ref[:, d:] = places[:m]
    both_ref[:, d:] = places


def pack(row_place, cache_len, group_place, cache_hidden, group_hidden):
    n, d = cache_hidden.shape
    m = TURN + PART
    args = (row_place.reshape(1, n), cache_len.reshape(1, -1), group_place.reshape(1, -1), cache_hidden, group_hidden)
    return pl.pallas_call(
        pack_kernel,
        in_specs=[VMEM] * 5,
        out_specs=[VMEM] * 3,
        out_shape=[jax.ShapeDtypeStruct(s, BF16) for s in ((m, d + HD), (REST, d), (m + REST, d + HD))],
        compiler_params=limit(56),
        cost_estimate=pl.CostEstimate(flops=2 * n * LIVE * d, bytes_accessed=4 * n * d, transcendentals=0),
        name="pack_live",
    )(*args)


def stage_kernel(in_ref, out_ref):
    out_ref[...] = in_ref[...]


def stage(x):
    return pl.pallas_call(
        stage_kernel,
        in_specs=[VMEM],
        out_specs=VMEM,
        out_shape=jax.ShapeDtypeStruct(x.shape, x.dtype),
        compiler_params=limit(8),
        cost_estimate=pl.CostEstimate(flops=0, bytes_accessed=4 * x.size, transcendentals=0),
        name="stage_rows",
    )(x)


def join_kernel(turns, own, up, down, far, out_ref):
    m, w = up.shape
    half = slice(0, m) if turns else slice(own.shape[0] - m, own.shape[0])
    x = [own[...].astype(F32)[half, :w], up[...].astype(F32), down[...].astype(F32)[half, :w], far[...].astype(F32)]
    n = len(x) * turns
    if turns:
        out_ref[:n] = jnp.concatenate([v[:turns] for v in x], axis=0).astype(BF16)
    out_ref[n:] = jnp.concatenate([v[turns:] for v in x], axis=0).astype(BF16)


def join(turns, *parts):
    m, w = parts[1].shape
    n = len(parts) * m
    return pl.pallas_call(
        functools.partial(join_kernel, turns),
        in_specs=[VMEM] * len(parts),
        out_specs=VMEM,
        out_shape=jax.ShapeDtypeStruct((n, w), BF16),
        compiler_params=limit(8),
        cost_estimate=pl.CostEstimate(flops=0, bytes_accessed=4 * n * w, transcendentals=0),
        name="join_shards",
    )(*parts)


def split_kernel(in_ref, turn_ref, rows_ref):
    n = turn_ref.shape[0]
    turn_ref[...] = in_ref[:n]
    rows_ref[...] = in_ref[n:, : rows_ref.shape[1]]


def split(block):
    m, w = block.shape
    n = 4 * TURN
    return pl.pallas_call(
        split_kernel,
        in_specs=[VMEM],
        out_specs=[VMEM] * 2,
        out_shape=[jax.ShapeDtypeStruct((n, w), BF16), jax.ShapeDtypeStruct((m - n, w - HD), BF16)],
        compiler_params=limit(8),
        cost_estimate=pl.CostEstimate(flops=0, bytes_accessed=4 * m * w, transcendentals=0),
        name="split_block",
    )(block)


def project_rows(refs, own_ref, other_ref):
    d = own_ref.shape[1]
    x = [r[4 * TURN :, :d] if r.shape[1] > d else r[...] for r in refs]
    w = jnp.concatenate([own_ref[1], own_ref[2], other_ref[1], other_ref[2]], axis=1)
    return jnp.dot(jnp.concatenate(x, axis=0), w, preferred_element_type=F32).astype(BF16)


def turn_kernel(*refs):
    *blocks, own_ref, other_ref, q_ref, kv_ref = refs
    d = own_ref.shape[1]
    turns = jnp.concatenate([r[: 4 * TURN] for r in blocks], axis=0)
    x = turns[:, :d]
    wq = jnp.concatenate([own_ref[0], other_ref[0]], axis=1)
    q_ref[:, : 2 * HD] = jnp.dot(x, wq, preferred_element_type=F32).astype(BF16)
    q_ref[:, 2 * HD :] = turns[:, d:]
    w = jnp.concatenate([own_ref[1], own_ref[2], other_ref[1], other_ref[2]], axis=1)
    kv_ref[...] = jnp.dot(x, w, preferred_element_type=F32).astype(BF16)


def turn_project(blocks, own, other):
    m, d = 16 * TURN, own.shape[1]
    return pl.pallas_call(
        turn_kernel,
        in_specs=[VMEM] * (len(blocks) + 2),
        out_specs=[VMEM] * 2,
        out_shape=[jax.ShapeDtypeStruct((m, 3 * HD), BF16), jax.ShapeDtypeStruct((m, 4 * HD), BF16)],
        compiler_params=limit(16),
        cost_estimate=pl.CostEstimate(flops=2 * m * d * 6 * HD * 6, bytes_accessed=2**20, transcendentals=0),
        name="project_turn",
    )(*blocks, own, other)


def cache_kernel(*refs):
    *rows, own_ref, other_ref, kv_ref = refs
    kv_ref[...] = project_rows(rows, own_ref, other_ref)


def cache_project(rows, own, other):
    m, d = 2 * LIVE * len(rows), own.shape[1]
    return pl.pallas_call(
        cache_kernel,
        in_specs=[VMEM] * (len(rows) + 2),
        out_specs=VMEM,
        out_shape=jax.ShapeDtypeStruct((m, 4 * HD), BF16),
        compiler_params=limit(16),
        cost_estimate=pl.CostEstimate(flops=2 * m * d * 4 * HD, bytes_accessed=2**20, transcendentals=0),
        name="project_cache",
    )(*rows, own, other)


def terms(x):
    hi = x.astype(BF16).astype(F32)
    mid = (x - hi).astype(BF16).astype(F32)
    return [hi, mid, x - hi - mid]


def scores_of(mine, theirs, h, keys):
    q = jnp.concatenate([mine[:, h * HD : (h + 1) * HD], theirs[:, (1 - h) * HD : (2 - h) * HD]], axis=0)
    nt = (((1,), (1,)), ((), ()))
    return lax.dot_general(q, keys, nt, preferred_element_type=F32) * HD ** (-0.5)


def key_value(block, h):
    return block[:, 2 * h * HD : (2 * h + 1) * HD], block[:, (2 * h + 1) * HD : (2 * h + 2) * HD]


def begin_kernel(q_ref, qs_ref, kvf_ref, *refs):
    *cache, sum_ref, top_ref, total_ref = refs
    mine, theirs, fresh = q_ref[...], qs_ref[...], kvf_ref[...]
    q_place = jnp.concatenate([mine[:, 2 * HD :], theirs[:, 2 * HD :]], axis=0).astype(F32)
    k_place = mine[:, 2 * HD :].astype(F32).T[0:1, :]
    seen = k_place <= q_place[:, 0:1]
    for h in range(2):
        pairs = [key_value(r[...], h) for r in cache] + [key_value(fresh, h)]
        s = [scores_of(mine, theirs, h, k) for k, _ in pairs]
        s[-1] = jnp.where(seen, s[-1], MASKED_SCORE)
        top = functools.reduce(jnp.maximum, [jnp.max(t, axis=1, keepdims=True) for t in s])
        total = jnp.zeros_like(top)
        summed = jnp.zeros((top.shape[0], HD), F32)
        for t, (_, v) in zip(s, pairs):
            e = jnp.exp(t - top)
            total += jnp.sum(e, axis=1, keepdims=True)
            summed += jnp.dot(e.astype(BF16), v, preferred_element_type=F32)
        sum_ref[h] = summed
        top_ref[h] = jnp.broadcast_to(top, summed.shape)
        total_ref[h] = jnp.broadcast_to(total, summed.shape)


def begin_attention(*arrays):
    tokens, keys = 2 * arrays[0].shape[0], sum(v.shape[0] for v in arrays[2:])
    return pl.pallas_call(
        begin_kernel,
        in_specs=[VMEM] * len(arrays),
        out_specs=[VMEM] * 3,
        out_shape=[jax.ShapeDtypeStruct((2, tokens, HD), F32)] * 3,
        compiler_params=limit(12),
        cost_estimate=pl.CostEstimate(
            flops=8 * tokens * keys * HD, bytes_accessed=2 * 2**20, transcendentals=2 * tokens * keys
        ),
        name="attend_begin",
    )(*arrays)


def end_kernel(q_ref, qs_ref, sum_ref, top_ref, total_ref, *refs):
    *rows, own_ref, other_ref, out_ref = refs
    me = lax.axis_index("seq")
    first = lax.rem(me, 2) == 0
    kv = project_rows(rows, own_ref, other_ref)
    mine, theirs = q_ref[...], qs_ref[...]
    tokens = sum_ref.shape[1]
    lane = lax.broadcasted_iota(jnp.int32, (tokens, HD), 1)
    outs, stats = [], []
    for h in range(2):
        keys, values = key_value(kv, h)
        s = scores_of(mine, theirs, h, keys)
        old = top_ref[h]
        top = jnp.maximum(old, jnp.max(s, axis=1, keepdims=True))
        e = jnp.exp(s - top[:, 0:1])
        scale = jnp.exp(old - top)
        total = total_ref[h] * scale + jnp.sum(e, axis=1, keepdims=True)
        outs.append(sum_ref[h] * scale + jnp.dot(e.astype(BF16), values, preferred_element_type=F32))
        stat = jnp.zeros((tokens, HD), F32)
        for i, v in enumerate(terms(top) + terms(total)):
            stat = jnp.where(lane % 64 // 8 == i, v, stat)
        stats.append(stat)
    low = jnp.where(first, outs[0], outs[1])
    high = jnp.where(first, outs[1], outs[0])
    stat = jnp.where((lane < 64) == first, stats[0], stats[1])
    whole = jnp.concatenate([low, high, stat], axis=1)
    for g in range(out_ref.shape[0]):
        out_ref[token_owner(me, g)] = whole[g * TURN : (g + 1) * TURN].astype(BF16)


def end_attention(*arrays):
    tokens, d, keys = 2 * arrays[0].shape[0], arrays[-1].shape[1], 4 * LIVE
    return pl.pallas_call(
        end_kernel,
        in_specs=[VMEM] * len(arrays),
        out_specs=VMEM,
        out_shape=jax.ShapeDtypeStruct((2 * NY * NX, TURN, 3 * HD), BF16),
        compiler_params=limit(16),
        cost_estimate=pl.CostEstimate(
            flops=8 * keys * HD * (d + tokens), bytes_accessed=2 * 2**20, transcendentals=2 * tokens * keys
        ),
        name="attend_end",
    )(*arrays)


def combine_kernel(in_ref, out_ref):
    for j in range(in_ref.shape[0] // 2):
        x = [in_ref[2 * j + i].astype(F32) for i in range(2)]
        stat = [v[:, 2 * HD :] for v in x]
        stat = [v + pltpu.roll(v, HD - 8, 1) + pltpu.roll(v, HD - 16, 1) for v in stat]
        total = [pltpu.roll(v, HD - 24, 1) for v in stat]
        top = jnp.maximum(*stat)
        scale = [jnp.exp(v - top) for v in stat]
        share = 1.0 / (total[0] * scale[0] + total[1] * scale[1])
        scale = [v * share for v in scale]
        for h in range(2):
            cols = slice(h * HD, (h + 1) * HD)
            out = sum(v[:, cols] * e[:, 64 * h : 64 * h + 1] for v, e in zip(x, scale))
            out_ref[:, (2 * j + h) * HD : (2 * j + h + 1) * HD] = out.astype(BF16)


def combine(parts):
    n, t, _ = parts.shape
    return pl.pallas_call(
        combine_kernel,
        out_shape=jax.ShapeDtypeStruct((t, n * HD), BF16),
        compiler_params=limit(4),
        cost_estimate=pl.CostEstimate(flops=n * t * HD * 8, bytes_accessed=n * t * HD * 14, transcendentals=n * t),
        name="combine",
    )(parts)


def shards(cache_hidden, group_hidden, proj_weight, row_place, cache_len, group_place):
    own = jnp.transpose(proj_weight[:, 0], (1, 0, 2))

    tie = lax.optimization_barrier
    one, two, both = pack(row_place, cache_len, group_place, cache_hidden, group_hidden)
    own, one, two, both = tie((own, one, two, both))
    one_up, two_up, down = send(one, A_UP), send(two, A_UP), send(both, A_DOWN)
    other = send(own, SWAP)
    one_up, staged = tie((one_up, stage(both)))
    first = join(TURN, staged, one_up, down, send(one_up, A_UP))
    second = join(0, staged, two_up, down, send(two_up, A_UP))
    first_down, second_up = send(first, B_DOWN), send(second, B_UP)
    second_down, first_up = send(second, B_DOWN), send(first, B_UP)
    first_down, second_up, other = tie((first_down, second_up, other))
    turn, rows = split(first_down)
    turn_far = send(turn, B_DOWN)
    far = send(rows, B_DOWN), send(second_up, B_UP)

    q, kv_turn = turn_project((first, first_up, first_down, turn_far), own, other)
    swapped = send(q, SWAP)
    kv = cache_project((first, second, first_up, second_up, first_down, second_down), own, other)
    begun = begin_attention(q, swapped, kv_turn, kv)
    *far, begun = tie((*far, begun))
    parts = end_attention(q, swapped, *begun, *far, own, other)
    landed = lax.all_to_all(parts, "seq", split_axis=0, concat_axis=0, tiled=True)
    return combine(landed)


def solution(mesh):
    in_specs = (
        P(("grp", "seq"), None),
        P(("grp", "seq"), None),
        P(None, "seq", None, None),
        P(("grp", "seq")),
        P("grp"),
        P(("grp", "seq")),
    )
    out_specs = P(("grp", "seq"), None)
    return jax.shard_map(shards, mesh=mesh, in_specs=in_specs, out_specs=out_specs, check_vma=False)
```

```python
import functools

import jax
import jax.numpy as jnp
from jax import lax
from jax.experimental import pallas as pl
from jax.experimental.pallas import tpu as pltpu
from jax.sharding import PartitionSpec as P

MASKED_SCORE = -1e30
NY, NX = 4, 4
LIVE = 48
HD = 128
TURN = 8
PART = 22
REST = LIVE - PART
BF16 = jnp.bfloat16
F32 = jnp.float32


def index_of(y, x, c):
    return (y % NY * NX + x % NX) * 2 + c


def ring_pairs(step, first):
    pairs = []
    for y in range(NY):
        for x in range(NX):
            for c in range(2):
                along_x = (c == 0) == first
                dy, dx = (0, step) if along_x else (step, 0)
                pairs.append((index_of(y, x, c), index_of(y + dy, x + dx, c)))
    return pairs


A_UP, A_DOWN = ring_pairs(1, False), ring_pairs(-1, False)
B_UP, B_DOWN = ring_pairs(1, True), ring_pairs(-1, True)
SWAP = [(i, i ^ 1) for i in range(2 * NY * NX)]
OFFSETS = (0, -1, 1, -2)


def token_owner(me, group):
    core = lax.rem(me, 2)
    y, x = lax.div(me, 2 * NX), lax.rem(lax.div(me, 2), NX)
    along_x = core == 1
    if group >= NX * NY:
        core, along_x = 1 - core, core == 0
    b, a = OFFSETS[group % (NX * NY) // 4], OFFSETS[group % 4]
    dy, dx = jnp.where(along_x, b, a), jnp.where(along_x, a, b)
    return (lax.rem(y + dy + NY, NY) * NX + lax.rem(x + dx + NX, NX)) * 2 + core


def send(value, pairs):
    return lax.ppermute(value, "seq", pairs)


VMEM = pl.BlockSpec(memory_space=pltpu.VMEM)


def limit(mib):
    return pltpu.CompilerParams(vmem_limit_bytes=mib * 2**20)


def pack_kernel(place_ref, len_ref, turn_place_ref, rows_ref, turn_ref, one_ref, two_ref):
    n, d = rows_ref.shape
    i0 = lax.broadcasted_iota(jnp.int32, (n, n), 0)
    i1 = lax.broadcasted_iota(jnp.int32, (n, n), 1)
    place_col = jnp.sum(jnp.where(i0 == i1, place_ref[...], 0), axis=1, keepdims=True)
    owner = place_col // n
    inner = place_col - owner * n
    o1 = lax.broadcasted_iota(jnp.int32, (n, len_ref.shape[1]), 1)
    length = jnp.sum(jnp.where(o1 == owner, len_ref[...], 0), axis=1, keepdims=True)
    live_col = (inner < length).astype(jnp.int32)
    live_row = jnp.sum(jnp.where(i0 == i1, live_col, 0), axis=0, keepdims=True)
    rank_row = jnp.sum(jnp.where(i0 < i1, live_col, 0), axis=0, keepdims=True)
    rank_row = jnp.where(live_row > 0, rank_row, -1)
    k0 = lax.broadcasted_iota(jnp.int32, (LIVE, n), 0)
    pick = jnp.where(k0 == rank_row, 1.0, 0.0).astype(BF16)
    live = jnp.dot(pick, rows_ref[...], preferred_element_type=F32)
    two_ref[...] = live[PART:].astype(BF16)
    rows = jnp.concatenate([turn_ref[...].astype(F32), live[:PART]], axis=0).astype(BF16)
    m = TURN + PART
    one_ref[:, :d] = rows
    t0 = lax.broadcasted_iota(jnp.int32, (m, TURN), 0)
    t1 = lax.broadcasted_iota(jnp.int32, (m, TURN), 1)
    turn_col = jnp.sum(jnp.where(t0 == t1, turn_place_ref[...], 0), axis=1, keepdims=True)
    places = jnp.broadcast_to(turn_col.astype(F32), (m, HD)).astype(BF16)
    one_ref[:, d:] = places


def pack(row_place, cache_len, group_place, cache_hidden, group_hidden):
    n, d = cache_hidden.shape
    m = TURN + PART
    args = (row_place.reshape(1, n), cache_len.reshape(1, -1), group_place.reshape(1, -1), cache_hidden, group_hidden)
    return pl.pallas_call(
        pack_kernel,
        in_specs=[VMEM] * 5,
        out_specs=[VMEM] * 2,
        out_shape=[jax.ShapeDtypeStruct(s, BF16) for s in ((m, d + HD), (REST, d))],
        compiler_params=limit(56),
        cost_estimate=pl.CostEstimate(flops=2 * n * LIVE * d, bytes_accessed=4 * n * d, transcendentals=0),
        name="pack_live",
    )(*args)


def stage_kernel(a, b, out_a, out_b):
    out_a[...] = a[...]
    out_b[...] = b[...]


def stage(*x):
    return pl.pallas_call(
        stage_kernel,
        in_specs=[VMEM] * 2,
        out_specs=[VMEM] * 2,
        out_shape=[jax.ShapeDtypeStruct(v.shape, v.dtype) for v in x],
        compiler_params=limit(8),
        cost_estimate=pl.CostEstimate(flops=0, bytes_accessed=4 * sum(v.size for v in x), transcendentals=0),
        name="stage_rows",
    )(*x)


def join_kernel(turns, own, up, down, far, out_ref):
    x = [r[...].astype(F32) for r in (own, up, down, far)]
    n = len(x) * turns
    if turns:
        out_ref[:n] = jnp.concatenate([v[:turns] for v in x], axis=0).astype(BF16)
    out_ref[n:] = jnp.concatenate([v[turns:] for v in x], axis=0).astype(BF16)


def join(turns, *parts):
    m, w = parts[1].shape
    n = len(parts) * m
    return pl.pallas_call(
        functools.partial(join_kernel, turns),
        in_specs=[VMEM] * len(parts),
        out_specs=VMEM,
        out_shape=jax.ShapeDtypeStruct((n, w), BF16),
        compiler_params=limit(8),
        cost_estimate=pl.CostEstimate(flops=0, bytes_accessed=4 * n * w, transcendentals=0),
        name="join_shards",
    )(*parts)


def split_kernel(in_ref, turn_ref, rows_ref):
    n = turn_ref.shape[0]
    turn_ref[...] = in_ref[:n]
    rows_ref[...] = in_ref[n:, : rows_ref.shape[1]]


def split(block):
    m, w = block.shape
    n = 4 * TURN
    return pl.pallas_call(
        split_kernel,
        in_specs=[VMEM],
        out_specs=[VMEM] * 2,
        out_shape=[jax.ShapeDtypeStruct((n, w), BF16), jax.ShapeDtypeStruct((m - n, w - HD), BF16)],
        compiler_params=limit(8),
        cost_estimate=pl.CostEstimate(flops=0, bytes_accessed=4 * m * w, transcendentals=0),
        name="split_block",
    )(block)


def project_rows(refs, own_ref, other_ref):
    d = own_ref.shape[1]
    x = [r[4 * TURN :, :d] if r.shape[1] > d else r[...] for r in refs]
    w = jnp.concatenate([own_ref[1], own_ref[2], other_ref[1], other_ref[2]], axis=1)
    return jnp.dot(jnp.concatenate(x, axis=0), w, preferred_element_type=F32).astype(BF16)


def turn_kernel(*refs):
    *blocks, own_ref, other_ref, q_ref, kv_ref = refs
    d = own_ref.shape[1]
    turns = jnp.concatenate([r[: 4 * TURN] for r in blocks], axis=0)
    x = turns[:, :d]
    wq = jnp.concatenate([own_ref[0], other_ref[0]], axis=1)
    q_ref[:, : 2 * HD] = jnp.dot(x, wq, preferred_element_type=F32).astype(BF16)
    q_ref[:, 2 * HD :] = turns[:, d:]
    w = jnp.concatenate([own_ref[1], own_ref[2], other_ref[1], other_ref[2]], axis=1)
    kv_ref[...] = jnp.dot(x, w, preferred_element_type=F32).astype(BF16)


def turn_project(blocks, own, other):
    m, d = 16 * TURN, own.shape[1]
    return pl.pallas_call(
        turn_kernel,
        in_specs=[VMEM] * (len(blocks) + 2),
        out_specs=[VMEM] * 2,
        out_shape=[jax.ShapeDtypeStruct((m, 3 * HD), BF16), jax.ShapeDtypeStruct((m, 4 * HD), BF16)],
        compiler_params=limit(16),
        cost_estimate=pl.CostEstimate(flops=2 * m * d * 6 * HD * 6, bytes_accessed=2**20, transcendentals=0),
        name="project_turn",
    )(*blocks, own, other)


def cache_kernel(*refs):
    *rows, own_ref, other_ref, kv_ref = refs
    kv_ref[...] = project_rows(rows, own_ref, other_ref)


def cache_project(rows, own, other):
    m, d = 2 * LIVE * len(rows), own.shape[1]
    return pl.pallas_call(
        cache_kernel,
        in_specs=[VMEM] * (len(rows) + 2),
        out_specs=VMEM,
        out_shape=jax.ShapeDtypeStruct((m, 4 * HD), BF16),
        compiler_params=limit(16),
        cost_estimate=pl.CostEstimate(flops=2 * m * d * 4 * HD, bytes_accessed=2**20, transcendentals=0),
        name="project_cache",
    )(*rows, own, other)


def terms(x):
    hi = x.astype(BF16).astype(F32)
    mid = (x - hi).astype(BF16).astype(F32)
    return [hi, mid, x - hi - mid]


def scores_of(mine, theirs, h, keys):
    q = jnp.concatenate([mine[:, h * HD : (h + 1) * HD], theirs[:, (1 - h) * HD : (2 - h) * HD]], axis=0)
    nt = (((1,), (1,)), ((), ()))
    return lax.dot_general(q, keys, nt, preferred_element_type=F32) * HD ** (-0.5)


def key_value(block, h):
    return block[:, 2 * h * HD : (2 * h + 1) * HD], block[:, (2 * h + 1) * HD : (2 * h + 2) * HD]


def begin_kernel(q_ref, qs_ref, kvf_ref, *refs):
    *cache, sum_ref, top_ref, total_ref = refs
    mine, theirs, fresh = q_ref[...], qs_ref[...], kvf_ref[...]
    q_place = jnp.concatenate([mine[:, 2 * HD :], theirs[:, 2 * HD :]], axis=0).astype(F32)
    k_place = mine[:, 2 * HD :].astype(F32).T[0:1, :]
    seen = k_place <= q_place[:, 0:1]
    for h in range(2):
        pairs = [key_value(r[...], h) for r in cache] + [key_value(fresh, h)]
        s = [scores_of(mine, theirs, h, k) for k, _ in pairs]
        s[-1] = jnp.where(seen, s[-1], MASKED_SCORE)
        top = functools.reduce(jnp.maximum, [jnp.max(t, axis=1, keepdims=True) for t in s])
        total = jnp.zeros_like(top)
        summed = jnp.zeros((top.shape[0], HD), F32)
        for t, (_, v) in zip(s, pairs):
            e = jnp.exp(t - top)
            total += jnp.sum(e, axis=1, keepdims=True)
            summed += jnp.dot(e.astype(BF16), v, preferred_element_type=F32)
        sum_ref[h] = summed
        top_ref[h] = jnp.broadcast_to(top, summed.shape)
        total_ref[h] = jnp.broadcast_to(total, summed.shape)


def begin_attention(*arrays):
    tokens, keys = 2 * arrays[0].shape[0], sum(v.shape[0] for v in arrays[2:])
    return pl.pallas_call(
        begin_kernel,
        in_specs=[VMEM] * len(arrays),
        out_specs=[VMEM] * 3,
        out_shape=[jax.ShapeDtypeStruct((2, tokens, HD), F32)] * 3,
        compiler_params=limit(12),
        cost_estimate=pl.CostEstimate(
            flops=8 * tokens * keys * HD, bytes_accessed=2 * 2**20, transcendentals=2 * tokens * keys
        ),
        name="attend_begin",
    )(*arrays)


def end_kernel(q_ref, qs_ref, sum_ref, top_ref, total_ref, *refs):
    *rows, own_ref, other_ref, out_ref = refs
    me = lax.axis_index("seq")
    first = lax.rem(me, 2) == 0
    kv = project_rows(rows, own_ref, other_ref)
    mine, theirs = q_ref[...], qs_ref[...]
    tokens = sum_ref.shape[1]
    lane = lax.broadcasted_iota(jnp.int32, (tokens, HD), 1)
    outs, stats = [], []
    for h in range(2):
        keys, values = key_value(kv, h)
        s = scores_of(mine, theirs, h, keys)
        old = top_ref[h]
        top = jnp.maximum(old, jnp.max(s, axis=1, keepdims=True))
        e = jnp.exp(s - top[:, 0:1])
        scale = jnp.exp(old - top)
        total = total_ref[h] * scale + jnp.sum(e, axis=1, keepdims=True)
        outs.append(sum_ref[h] * scale + jnp.dot(e.astype(BF16), values, preferred_element_type=F32))
        stat = jnp.zeros((tokens, HD), F32)
        for i, v in enumerate(terms(top) + terms(total)):
            stat = jnp.where(lane % 64 // 8 == i, v, stat)
        stats.append(stat)
    low = jnp.where(first, outs[0], outs[1])
    high = jnp.where(first, outs[1], outs[0])
    stat = jnp.where((lane < 64) == first, stats[0], stats[1])
    whole = jnp.concatenate([low, high, stat], axis=1)
    for g in range(out_ref.shape[0]):
        out_ref[token_owner(me, g)] = whole[g * TURN : (g + 1) * TURN].astype(BF16)


def end_attention(*arrays):
    tokens, d, keys = 2 * arrays[0].shape[0], arrays[-1].shape[1], 4 * LIVE
    return pl.pallas_call(
        end_kernel,
        in_specs=[VMEM] * len(arrays),
        out_specs=VMEM,
        out_shape=jax.ShapeDtypeStruct((2 * NY * NX, TURN, 3 * HD), BF16),
        compiler_params=limit(16),
        cost_estimate=pl.CostEstimate(
            flops=8 * keys * HD * (d + tokens), bytes_accessed=2 * 2**20, transcendentals=2 * tokens * keys
        ),
        name="attend_end",
    )(*arrays)


def combine_kernel(in_ref, out_ref):
    for j in range(in_ref.shape[0] // 2):
        x = [in_ref[2 * j + i].astype(F32) for i in range(2)]
        stat = [v[:, 2 * HD :] for v in x]
        stat = [v + pltpu.roll(v, HD - 8, 1) + pltpu.roll(v, HD - 16, 1) for v in stat]
        total = [pltpu.roll(v, HD - 24, 1) for v in stat]
        top = jnp.maximum(*stat)
        scale = [jnp.exp(v - top) for v in stat]
        share = 1.0 / (total[0] * scale[0] + total[1] * scale[1])
        scale = [v * share for v in scale]
        for h in range(2):
            cols = slice(h * HD, (h + 1) * HD)
            out = sum(v[:, cols] * e[:, 64 * h : 64 * h + 1] for v, e in zip(x, scale))
            out_ref[:, (2 * j + h) * HD : (2 * j + h + 1) * HD] = out.astype(BF16)


def combine(parts):
    n, t, _ = parts.shape
    return pl.pallas_call(
        combine_kernel,
        out_shape=jax.ShapeDtypeStruct((t, n * HD), BF16),
        compiler_params=limit(4),
        cost_estimate=pl.CostEstimate(flops=n * t * HD * 8, bytes_accessed=n * t * HD * 14, transcendentals=n * t),
        name="combine",
    )(parts)


def shards(cache_hidden, group_hidden, proj_weight, row_place, cache_len, group_place):
    own = jnp.transpose(proj_weight[:, 0], (1, 0, 2))

    tie = lax.optimization_barrier
    one, two = pack(row_place, cache_len, group_place, cache_hidden, group_hidden)
    own, one, two = tie((own, one, two))
    one_up, one_down = send(one, A_UP), send(one, A_DOWN)
    two_up, two_down = send(two, A_UP), send(two, A_DOWN)
    other = send(own, SWAP)
    one_up, one, two = tie((one_up, *stage(one, two)))
    first = join(TURN, one, one_up, one_down, send(one_up, A_UP))
    second = join(0, two, two_up, two_down, send(two_down, A_DOWN))
    first_down, second_up = send(first, B_DOWN), send(second, B_UP)
    second_down, first_up = send(second, B_DOWN), send(first, B_UP)
    first_down, second_up, other = tie((first_down, second_up, other))
    turn, rows = split(first_down)
    turn_far = send(turn, B_DOWN)
    far = send(rows, B_DOWN), send(second_up, B_UP)

    q, kv_turn = turn_project((first, first_up, first_down, turn_far), own, other)
    swapped = send(q, SWAP)
    kv = cache_project((first, second, first_up, second_up, first_down, second_down), own, other)
    begun = begin_attention(q, swapped, kv_turn, kv)
    *far, begun = tie((*far, begun))
    parts = end_attention(q, swapped, *begun, *far, own, other)
    landed = lax.all_to_all(parts, "seq", split_axis=0, concat_axis=0, tiled=True)
    return combine(landed)


def solution(mesh):
    in_specs = (
        P(("grp", "seq"), None),
        P(("grp", "seq"), None),
        P(None, "seq", None, None),
        P(("grp", "seq")),
        P("grp"),
        P(("grp", "seq")),
    )
    out_specs = P(("grp", "seq"), None)
    return jax.shard_map(shards, mesh=mesh, in_specs=in_specs, out_specs=out_specs, check_vma=False)
```

```python
import functools

import jax
import jax.numpy as jnp
from jax import lax
from jax.experimental import pallas as pl
from jax.experimental.pallas import tpu as pltpu
from jax.sharding import PartitionSpec as P

MASKED_SCORE = -1e30
NY, NX = 4, 4
LIVE = 48
HD = 128
TURN = 8
PART = 22
REST = LIVE - PART
BF16 = jnp.bfloat16
F32 = jnp.float32


def index_of(y, x, c):
    return (y % NY * NX + x % NX) * 2 + c


def ring_pairs(step, first):
    pairs = []
    for y in range(NY):
        for x in range(NX):
            for c in range(2):
                along_x = (c == 0) == first
                dy, dx = (0, step) if along_x else (step, 0)
                pairs.append((index_of(y, x, c), index_of(y + dy, x + dx, c)))
    return pairs


A_UP, A_DOWN = ring_pairs(1, False), ring_pairs(-1, False)
B_UP, B_DOWN = ring_pairs(1, True), ring_pairs(-1, True)
SWAP = [(i, i ^ 1) for i in range(2 * NY * NX)]
OFFSETS = (0, -1, 1, -2)


def token_owner(me, group):
    core = lax.rem(me, 2)
    y, x = lax.div(me, 2 * NX), lax.rem(lax.div(me, 2), NX)
    along_x = core == 1
    if group >= NX * NY:
        core, along_x = 1 - core, core == 0
    b, a = OFFSETS[group % (NX * NY) // 4], OFFSETS[group % 4]
    dy, dx = jnp.where(along_x, b, a), jnp.where(along_x, a, b)
    return (lax.rem(y + dy + NY, NY) * NX + lax.rem(x + dx + NX, NX)) * 2 + core


def send(value, pairs):
    return lax.ppermute(value, "seq", pairs)


VMEM = pl.BlockSpec(memory_space=pltpu.VMEM)


def limit(mib):
    return pltpu.CompilerParams(vmem_limit_bytes=mib * 2**20)


def pack_kernel(place_ref, len_ref, turn_place_ref, rows_ref, turn_ref, one_ref, two_ref, both_ref):
    n, d = rows_ref.shape
    i0 = lax.broadcasted_iota(jnp.int32, (n, n), 0)
    i1 = lax.broadcasted_iota(jnp.int32, (n, n), 1)
    place_col = jnp.sum(jnp.where(i0 == i1, place_ref[...], 0), axis=1, keepdims=True)
    owner = lax.shift_right_logical(place_col, n.bit_length() - 1)
    inner = place_col & (n - 1)
    o1 = lax.broadcasted_iota(jnp.int32, (n, len_ref.shape[1]), 1)
    length = jnp.sum(jnp.where(o1 == owner, len_ref[...], 0), axis=1, keepdims=True)
    live_col = (inner < length).astype(jnp.int32)
    live_row = jnp.sum(jnp.where(i0 == i1, live_col, 0), axis=0, keepdims=True)
    rank_row = jnp.sum(jnp.where(i0 < i1, live_col, 0), axis=0, keepdims=True)
    rank_row = jnp.where(live_row > 0, rank_row, -1)
    k0 = lax.broadcasted_iota(jnp.int32, (LIVE, n), 0)
    pick = jnp.where(k0 == rank_row, 1.0, 0.0).astype(BF16)
    live = jnp.dot(pick, rows_ref[...], preferred_element_type=F32)
    two_ref[...] = live[PART:].astype(BF16)
    rows = jnp.concatenate([turn_ref[...].astype(F32), live], axis=0).astype(BF16)
    m = TURN + PART
    one_ref[:, :d] = rows[:m]
    both_ref[:, :d] = rows
    t0 = lax.broadcasted_iota(jnp.int32, (TURN + LIVE, TURN), 0)
    t1 = lax.broadcasted_iota(jnp.int32, (TURN + LIVE, TURN), 1)
    turn_col = jnp.sum(jnp.where(t0 == t1, turn_place_ref[...], 0), axis=1, keepdims=True)
    places = jnp.broadcast_to(turn_col.astype(F32), (TURN + LIVE, HD)).astype(BF16)
    one_ref[:, d:] = places[:m]
    both_ref[:, d:] = places


def pack(row_place, cache_len, group_place, cache_hidden, group_hidden):
    n, d = cache_hidden.shape
    m = TURN + PART
    args = (row_place.reshape(1, n), cache_len.reshape(1, -1), group_place.reshape(1, -1), cache_hidden, group_hidden)
    return pl.pallas_call(
        pack_kernel,
        in_specs=[VMEM] * 5,
        out_specs=[VMEM] * 3,
        out_shape=[jax.ShapeDtypeStruct(s, BF16) for s in ((m, d + HD), (REST, d), (m + REST, d + HD))],
        compiler_params=limit(56),
        cost_estimate=pl.CostEstimate(flops=2 * n * LIVE * d, bytes_accessed=4 * n * d, transcendentals=0),
        name="pack_live",
    )(*args)


def stage_kernel(in_ref, out_ref):
    out_ref[...] = in_ref[...]


def stage(x):
    return pl.pallas_call(
        stage_kernel,
        in_specs=[VMEM],
        out_specs=VMEM,
        out_shape=jax.ShapeDtypeStruct(x.shape, x.dtype),
        compiler_params=limit(8),
        cost_estimate=pl.CostEstimate(flops=0, bytes_accessed=4 * x.size, transcendentals=0),
        name="stage_rows",
    )(x)


def join_kernel(turns, own, up, down, far, out_ref):
    m, w = up.shape
    half = slice(0, m) if turns else slice(own.shape[0] - m, own.shape[0])
    x = [own[...].astype(F32)[half, :w], up[...].astype(F32), down[...].astype(F32)[half, :w], far[...].astype(F32)]
    n = len(x) * turns
    if turns:
        out_ref[:n] = jnp.concatenate([v[:turns] for v in x], axis=0).astype(BF16)
    out_ref[n:] = jnp.concatenate([v[turns:] for v in x], axis=0).astype(BF16)


def join(turns, *parts):
    m, w = parts[1].shape
    n = len(parts) * m
    return pl.pallas_call(
        functools.partial(join_kernel, turns),
        in_specs=[VMEM] * len(parts),
        out_specs=VMEM,
        out_shape=jax.ShapeDtypeStruct((n, w), BF16),
        compiler_params=limit(8),
        cost_estimate=pl.CostEstimate(flops=0, bytes_accessed=4 * n * w, transcendentals=0),
        name="join_shards",
    )(*parts)


def split_kernel(in_ref, turn_ref, rows_ref):
    n = turn_ref.shape[0]
    turn_ref[...] = in_ref[:n]
    rows_ref[...] = in_ref[n:, : rows_ref.shape[1]]


def split(block):
    m, w = block.shape
    n = 4 * TURN
    return pl.pallas_call(
        split_kernel,
        in_specs=[VMEM],
        out_specs=[VMEM] * 2,
        out_shape=[jax.ShapeDtypeStruct((n, w), BF16), jax.ShapeDtypeStruct((m - n, w - HD), BF16)],
        compiler_params=limit(8),
        cost_estimate=pl.CostEstimate(flops=0, bytes_accessed=4 * m * w, transcendentals=0),
        name="split_block",
    )(block)


def project_rows(refs, own_ref, other_ref):
    d = own_ref.shape[1]
    x = [r[4 * TURN :, :d] if r.shape[1] > d else r[...] for r in refs]
    w = jnp.concatenate([own_ref[1], own_ref[2], other_ref[1], other_ref[2]], axis=1)
    return jnp.dot(jnp.concatenate(x, axis=0), w, preferred_element_type=F32).astype(BF16)


def turn_kernel(*refs):
    *blocks, own_ref, other_ref, q_ref, kv_ref = refs
    d = own_ref.shape[1]
    turns = jnp.concatenate([r[: 4 * TURN] for r in blocks], axis=0)
    x = turns[:, :d]
    wq = jnp.concatenate([own_ref[0], other_ref[0]], axis=1)
    q_ref[:, : 2 * HD] = jnp.dot(x, wq, preferred_element_type=F32).astype(BF16)
    q_ref[:, 2 * HD :] = turns[:, d:]
    w = jnp.concatenate([own_ref[1], own_ref[2], other_ref[1], other_ref[2]], axis=1)
    kv_ref[...] = jnp.dot(x, w, preferred_element_type=F32).astype(BF16)


def turn_project(blocks, own, other):
    m, d = 16 * TURN, own.shape[1]
    return pl.pallas_call(
        turn_kernel,
        in_specs=[VMEM] * (len(blocks) + 2),
        out_specs=[VMEM] * 2,
        out_shape=[jax.ShapeDtypeStruct((m, 3 * HD), BF16), jax.ShapeDtypeStruct((m, 4 * HD), BF16)],
        compiler_params=limit(16),
        cost_estimate=pl.CostEstimate(flops=2 * m * d * 6 * HD * 6, bytes_accessed=2**20, transcendentals=0),
        name="project_turn",
    )(*blocks, own, other)


def cache_kernel(*refs):
    *rows, own_ref, other_ref, kv_ref = refs
    kv_ref[...] = project_rows(rows, own_ref, other_ref)


def cache_project(rows, own, other):
    m, d = 2 * LIVE * len(rows), own.shape[1]
    return pl.pallas_call(
        cache_kernel,
        in_specs=[VMEM] * (len(rows) + 2),
        out_specs=VMEM,
        out_shape=jax.ShapeDtypeStruct((m, 4 * HD), BF16),
        compiler_params=limit(16),
        cost_estimate=pl.CostEstimate(flops=2 * m * d * 4 * HD, bytes_accessed=2**20, transcendentals=0),
        name="project_cache",
    )(*rows, own, other)


def terms(x):
    hi = x.astype(BF16).astype(F32)
    mid = (x - hi).astype(BF16).astype(F32)
    return [hi, mid, x - hi - mid]


def scores_of(mine, theirs, h, keys):
    q = jnp.concatenate([mine[:, h * HD : (h + 1) * HD], theirs[:, (1 - h) * HD : (2 - h) * HD]], axis=0)
    nt = (((1,), (1,)), ((), ()))
    return lax.dot_general(q, keys, nt, preferred_element_type=F32) * HD ** (-0.5)


def key_value(block, h):
    return block[:, 2 * h * HD : (2 * h + 1) * HD], block[:, (2 * h + 1) * HD : (2 * h + 2) * HD]


def begin_kernel(q_ref, qs_ref, kvf_ref, *refs):
    *cache, sum_ref, top_ref, total_ref = refs
    mine, theirs, fresh = q_ref[...], qs_ref[...], kvf_ref[...]
    q_place = jnp.concatenate([mine[:, 2 * HD :], theirs[:, 2 * HD :]], axis=0).astype(F32)
    k_place = mine[:, 2 * HD :].astype(F32).T[0:1, :]
    seen = k_place <= q_place[:, 0:1]
    for h in range(2):
        pairs = [key_value(r[...], h) for r in cache] + [key_value(fresh, h)]
        s = [scores_of(mine, theirs, h, k) for k, _ in pairs]
        s[-1] = jnp.where(seen, s[-1], MASKED_SCORE)
        top = functools.reduce(jnp.maximum, [jnp.max(t, axis=1, keepdims=True) for t in s])
        total = jnp.zeros_like(top)
        summed = jnp.zeros((top.shape[0], HD), F32)
        for t, (_, v) in zip(s, pairs):
            e = jnp.exp(t - top)
            total += jnp.sum(e, axis=1, keepdims=True)
            summed += jnp.dot(e.astype(BF16), v, preferred_element_type=F32)
        sum_ref[h] = summed
        top_ref[h] = jnp.broadcast_to(top, summed.shape)
        total_ref[h] = jnp.broadcast_to(total, summed.shape)


def begin_attention(*arrays):
    tokens, keys = 2 * arrays[0].shape[0], sum(v.shape[0] for v in arrays[2:])
    return pl.pallas_call(
        begin_kernel,
        in_specs=[VMEM] * len(arrays),
        out_specs=[VMEM] * 3,
        out_shape=[jax.ShapeDtypeStruct((2, tokens, HD), F32)] * 3,
        compiler_params=limit(12),
        cost_estimate=pl.CostEstimate(
            flops=8 * tokens * keys * HD, bytes_accessed=2 * 2**20, transcendentals=2 * tokens * keys
        ),
        name="attend_begin",
    )(*arrays)


def end_kernel(q_ref, qs_ref, sum_ref, top_ref, total_ref, *refs):
    *rows, own_ref, other_ref, out_ref = refs
    me = lax.axis_index("seq")
    first = lax.rem(me, 2) == 0
    kv = project_rows(rows, own_ref, other_ref)
    mine, theirs = q_ref[...], qs_ref[...]
    tokens = sum_ref.shape[1]
    lane = lax.broadcasted_iota(jnp.int32, (tokens, HD), 1)
    outs, stats = [], []
    for h in range(2):
        keys, values = key_value(kv, h)
        s = scores_of(mine, theirs, h, keys)
        old = top_ref[h]
        top = jnp.maximum(old, jnp.max(s, axis=1, keepdims=True))
        e = jnp.exp(s - top[:, 0:1])
        scale = jnp.exp(old - top)
        total = total_ref[h] * scale + jnp.sum(e, axis=1, keepdims=True)
        outs.append(sum_ref[h] * scale + jnp.dot(e.astype(BF16), values, preferred_element_type=F32))
        stat = jnp.zeros((tokens, HD), F32)
        for i, v in enumerate(terms(top) + terms(total)):
            stat = jnp.where(lane % 64 // 8 == i, v, stat)
        stats.append(stat)
    low = jnp.where(first, outs[0], outs[1])
    high = jnp.where(first, outs[1], outs[0])
    stat = jnp.where((lane < 64) == first, stats[0], stats[1])
    whole = jnp.concatenate([low, high, stat], axis=1)
    for g in range(out_ref.shape[0]):
        out_ref[token_owner(me, g)] = whole[g * TURN : (g + 1) * TURN].astype(BF16)


def end_attention(*arrays):
    tokens, d, keys = 2 * arrays[0].shape[0], arrays[-1].shape[1], 4 * LIVE
    return pl.pallas_call(
        end_kernel,
        in_specs=[VMEM] * len(arrays),
        out_specs=VMEM,
        out_shape=jax.ShapeDtypeStruct((2 * NY * NX, TURN, 3 * HD), BF16),
        compiler_params=limit(16),
        cost_estimate=pl.CostEstimate(
            flops=8 * keys * HD * (d + tokens), bytes_accessed=2 * 2**20, transcendentals=2 * tokens * keys
        ),
        name="attend_end",
    )(*arrays)


def combine_kernel(in_ref, out_ref):
    for j in range(in_ref.shape[0] // 2):
        x = [in_ref[2 * j + i].astype(F32) for i in range(2)]
        stat = [v[:, 2 * HD :] for v in x]
        stat = [v + pltpu.roll(v, HD - 8, 1) + pltpu.roll(v, HD - 16, 1) for v in stat]
        total = [pltpu.roll(v, HD - 24, 1) for v in stat]
        top = jnp.maximum(*stat)
        scale = [jnp.exp(v - top) for v in stat]
        share = 1.0 / (total[0] * scale[0] + total[1] * scale[1])
        scale = [v * share for v in scale]
        for h in range(2):
            cols = slice(h * HD, (h + 1) * HD)
            out = sum(v[:, cols] * e[:, 64 * h : 64 * h + 1] for v, e in zip(x, scale))
            out_ref[:, (2 * j + h) * HD : (2 * j + h + 1) * HD] = out.astype(BF16)


def combine(parts):
    n, t, _ = parts.shape
    return pl.pallas_call(
        combine_kernel,
        out_shape=jax.ShapeDtypeStruct((t, n * HD), BF16),
        compiler_params=limit(4),
        cost_estimate=pl.CostEstimate(flops=n * t * HD * 8, bytes_accessed=n * t * HD * 14, transcendentals=n * t),
        name="combine",
    )(parts)


def shards(cache_hidden, group_hidden, proj_weight, row_place, cache_len, group_place):
    own = jnp.transpose(proj_weight[:, 0], (1, 0, 2))

    tie = lax.optimization_barrier
    one, two, both = pack(row_place, cache_len, group_place, cache_hidden, group_hidden)
    own, one, two, both = tie((own, one, two, both))
    one_up, two_up, down = send(one, A_UP), send(two, A_UP), send(both, A_DOWN)
    other = send(own, SWAP)
    one_up, staged = tie((one_up, stage(both)))
    first = join(TURN, staged, one_up, down, send(one_up, A_UP))
    second = join(0, staged, two_up, down, send(two_up, A_UP))
    first_down, second_up = send(first, B_DOWN), send(second, B_UP)
    second_down, first_up = send(second, B_DOWN), send(first, B_UP)
    first_down, second_up, other = tie((first_down, second_up, other))
    turn, rows = split(first_down)
    turn_far = send(turn, B_DOWN)
    far = send(rows, B_DOWN), send(second_up, B_UP)

    q, kv_turn = turn_project((first, first_up, first_down, turn_far), own, other)
    swapped = send(q, SWAP)
    kv = cache_project((first, second, first_up, second_up, first_down, second_down), own, other)
    begun = begin_attention(q, swapped, kv_turn, kv)
    *far, begun = tie((*far, begun))
    parts = end_attention(q, swapped, *begun, *far, own, other)
    landed = lax.all_to_all(parts, "seq", split_axis=0, concat_axis=0, tiled=True)
    return combine(landed)


def solution(mesh):
    in_specs = (
        P(("grp", "seq"), None),
        P(("grp", "seq"), None),
        P(None, "seq", None, None),
        P(("grp", "seq")),
        P("grp"),
        P(("grp", "seq")),
    )
    out_specs = P(("grp", "seq"), None)
    return jax.shard_map(shards, mesh=mesh, in_specs=in_specs, out_specs=out_specs, check_vma=False)
```
